256 devices in a mesh: row: 4 (over z_hi, core), col: 16 (over z_lo, x), rep: 4 (over y).
Axes of the slice: x: 4, y: 4, z: 8 (z_hi: 2, z_lo: 4; z = z_hi * 4 + z_lo), core: 2. Of those that a mesh axis runs over, the one named last changes fastest.
Arguments:
- node_features: bfloat16 [32768, 256], P(('row', 'col', 'rep')), may hold values from -6 to 6
- cotangent: bfloat16 [32768, 256], P(('row', 'col', 'rep')), may hold values from -6 to 6
- w_first: bfloat16 [256, 512], replicated, may hold values from -0.375 to 0.375
- w_second: bfloat16 [512, 256], replicated, may hold values from -0.25 to 0.25
- tile_weights: bfloat16 [49152, 128, 128], P(('row', 'col', 'rep')), may hold values from 0 to 0.05, as said below
- tile_rows: int32 [49152], P(('row', 'col', 'rep')), may hold values from 0 to 63
- tile_cols: int32 [49152], P(('row', 'col', 'rep')), may hold values from 0 to 15
- tile_counts: int32 [256], P(('row', 'col', 'rep')), may hold values from 24 to 192, as said below
Outputs:
- grad_features: float32 [32768, 256], P(('row', 'col', 'rep'))
The draws below stay inside these ranges and needn't reach their ends.
Inputs may be any that keep to these rules, and one draw needn't show every extreme that they name: `tile_weights`: positive edge weights. Device d uses slots 0 to tile_counts[d] - 1 of its 192 slots; the other slots are not part of the graph; in every draw some device uses all 192 slots and some device an eighth of them.
All inputs are finite; a program needn't handle non-finite values.
Results may differ from the reference program's by a relative error of at most 0.0021.
The reference program's roundings to bfloat16 on the way count: a program that leaves them out, or rounds other values in their place, can miss the bound.
Values may be sent and summed in bfloat16 or wider, within the bound.
No kernel may reach another device: no remote copies, remote signals or barrier semaphores. Data moves between devices by JAX's collectives and lax.ppermute only.
A program may use at most 64 MiB of HBM per device.

```python
import jax
import jax.numpy as jnp
from jax import lax

H = 256
F = 512
TS = 128
ROWS = 128
TILES = 192
N_NODES = 32768
TILE_ALL = 49152
RB_TILES = 64
CB_TILES = 16
N_ROW = 4
N_COL = 16
N_REP = 4
DEVICES = 256


def draw_tile_weights(key, part):
    key = jax.random.fold_in(key, 11)
    first_key = jax.random.fold_in(key, 0)
    exponents = jax.random.uniform(first_key, (TILE_ALL, TS, TS), jnp.float32, -80.0, 0.0)
    values = 0.049 * jnp.exp(exponents)
    return values.astype(jnp.bfloat16)


def draw_tile_counts(key, part):
    key = jax.random.fold_in(key, 23)
    first_key, second_key = jax.random.split(key)
    raw_draw = jax.random.randint(first_key, (DEVICES,), 0, TILES + 1)
    counts = jnp.maximum(TILES // 8, raw_draw * raw_draw // TILES)
    order = jax.random.permutation(second_key, DEVICES)
    counts = counts.at[order[0]].set(TILES).at[order[1]].set(TILES // 8)
    return counts.astype(jnp.int32)


def set_ends(result, own_key, least, top_value):
    longest = result.shape.index(max(result.shape))
    spots = []
    for shift in (0, 1):
        where = [jax.random.randint(jax.random.fold_in(own_key, axis), (), 0, length) for axis, length in enumerate(result.shape)]
        where[longest] = (where[longest] + shift) % result.shape[longest]
        spots.append(tuple(where))
    return result.at[spots[0]].set(least).at[spots[1]].set(top_value)


def steps_of(stream_key, extent, cuts, smallest, high):
    def one(dim, blocks):
        draws = jax.random.uniform(jax.random.fold_in(jax.random.fold_in(stream_key, 6), dim), (blocks,), jnp.float32, smallest / len(cuts), high / len(cuts))
        return jnp.repeat(jnp.exp(draws), extent[dim] // blocks).reshape((-1,) + (1,) * (len(extent) - dim - 1))

    loudness = one(*cuts[0])
    for cut in cuts[1:]:
        loudness = loudness * one(*cut)
    return loudness


def gaussian(rng, dims, width, reach, cuts=(), held_as=jnp.bfloat16):
    gain = steps_of(rng, dims, cuts, -0.22, 0.18) if cuts else 1.0
    result = jax.random.normal(rng, dims, jnp.float32) * width * gain
    return jnp.minimum(jnp.maximum(result, -reach), reach).astype(held_as)


def setup_inputs(seed: int = 0) -> dict:
    seeds = jax.random.split(jax.random.key(seed), 9)
    return {
        "node_features": gaussian(seeds[0], (N_NODES, H), 1.0, 6.0, ((0, 256),)),
        "cotangent": gaussian(seeds[1], (N_NODES, H), 1.0, 6.0, ((0, 256),)),
        "w_first": gaussian(seeds[2], (H, F), H ** -0.5, 0.375),
        "w_second": gaussian(seeds[3], (F, H), F ** -0.5, 0.25),
        "tile_weights": draw_tile_weights(jax.random.fold_in(seeds[8], 71), 0),
        "tile_rows": set_ends(jax.random.randint(seeds[5], (TILE_ALL,), 0, RB_TILES), jax.random.fold_in(seeds[5], 1), 0, RB_TILES - 1).astype(jnp.int32),
        "tile_cols": set_ends(jax.random.randint(seeds[6], (TILE_ALL,), 0, CB_TILES), jax.random.fold_in(seeds[6], 1), 0, CB_TILES - 1).astype(jnp.int32),
        "tile_counts": draw_tile_counts(jax.random.fold_in(seeds[8], 71), 0),
    }


EXPONENT = 2.5


def node_terms(as_float, cotangent, powered, neighbour, degree, w_first, w_second):
    denominator = 1.0 + degree
    mean_pow = (powered + neighbour) / denominator[:, None]
    aggregated = jnp.exp(jnp.log(mean_pow) / EXPONENT)
    mixed_half = (aggregated + as_float).astype(jnp.bfloat16)
    pre_act = jnp.dot(mixed_half, w_first, preferred_element_type=jnp.float32)
    sigmoid_pre = jax.nn.sigmoid(pre_act)
    grad_act = jnp.dot(cotangent, w_second.T, preferred_element_type=jnp.float32)
    grad_pre = (grad_act * sigmoid_pre * (1.0 + pre_act * (1.0 - sigmoid_pre))).astype(jnp.bfloat16)
    grad_mixed = jnp.dot(grad_pre, w_first.T, preferred_element_type=jnp.float32)
    scaled = grad_mixed * aggregated / (EXPONENT * mean_pow) / denominator[:, None]
    return scaled, grad_mixed


def reference(node_features, cotangent, w_first, w_second, tile_weights, tile_rows, tile_cols, tile_counts):
    as_float = node_features.astype(jnp.float32)
    messages = jax.nn.softplus(as_float)
    powered = jnp.exp(EXPONENT * jnp.log(messages))
    powered_half = powered.astype(jnp.bfloat16)
    slot_index = jnp.arange(TILE_ALL, dtype=jnp.int32)
    owner = slot_index // TILES
    live_slot = (slot_index % TILES) < tile_counts[owner]
    global_rows = ((owner // (N_COL * N_REP)) * RB_TILES + tile_rows).astype(jnp.int32)
    global_cols = (((owner // N_REP) % N_COL) * CB_TILES + tile_cols).astype(jnp.int32)
    panels = powered_half.reshape(N_ROW, N_COL, N_REP, ROWS, H).transpose(1, 0, 2, 3, 4).reshape(N_COL * CB_TILES, TS, H)
    weight_shape = (DEVICES, TILES, TS, TS)
    index_shape = (DEVICES, TILES)
    stacked = (tile_weights.reshape(weight_shape), global_rows.reshape(index_shape), global_cols.reshape(index_shape), live_slot.reshape(index_shape))

    def forward_step(totals, slot_data):
        neighbour, degree = totals
        weights, rows_at, cols_at, keep_slot = slot_data
        weights = jnp.where(keep_slot[:, None, None], weights.astype(jnp.float32), jnp.float32(0.0))
        product = jnp.einsum("tij,tjh->tih", weights, panels[cols_at].astype(jnp.float32), precision=lax.Precision.HIGHEST)
        return (neighbour.at[rows_at].add(product), degree.at[rows_at].add(jnp.sum(weights, axis=2))), None

    initial = (jnp.zeros((N_ROW * RB_TILES, TS, H), jnp.float32), jnp.zeros((N_ROW * RB_TILES, TS), jnp.float32))
    (neighbour, degree), _ = lax.scan(forward_step, initial, stacked)
    neighbour = neighbour.reshape(N_NODES, H)
    degree = degree.reshape(N_NODES)
    scaled, grad_mixed = node_terms(as_float, cotangent, powered, neighbour, degree, w_first, w_second)
    row_source = scaled.astype(jnp.bfloat16).reshape(N_ROW * RB_TILES, TS, H)

    def backward_step(back_sums, slot_data):
        weights, rows_at, cols_at, keep_slot = slot_data
        weights = jnp.where(keep_slot[:, None, None], weights.astype(jnp.float32), jnp.float32(0.0))
        product = jnp.einsum("tij,tih->tjh", weights, row_source[rows_at].astype(jnp.float32), precision=lax.Precision.HIGHEST)
        return back_sums.at[cols_at].add(product), None

    back_sums, _ = lax.scan(backward_step, jnp.zeros((N_COL * CB_TILES, TS, H), jnp.float32), stacked)
    back_sums = back_sums.reshape(N_COL, N_ROW, N_REP, ROWS, H).transpose(1, 0, 2, 3, 4).reshape(N_NODES, H)
    grad_message = (scaled + back_sums) * (EXPONENT * powered / messages) * jax.nn.sigmoid(as_float)
    return cotangent.astype(jnp.float32) + grad_mixed + grad_message
```

```python
import jax
import jax.numpy as jnp
from jax import lax
from jax.experimental import pallas as pl
from jax.experimental.pallas import tpu as pltpu
from jax.sharding import Mesh
from jax.sharding import PartitionSpec as P

EXPONENT = 2.5
AXES = ("zh", "core", "zl", "x", "y")
TS = 128
H = 256
HALF = 128
CHUNK = 16
F32 = jnp.float32
BF16 = jnp.bfloat16
VMEM = pltpu.VMEM
MIB = 1 << 20


def shift(value, axis, step):
    return lax.ppermute(value, axis, [(i, (i + step) % 4) for i in range(4)])


def swap(value, axis):
    return lax.ppermute(value, axis, [(0, 1), (1, 0)])


def softplus(value):
    return jnp.maximum(value, 0.0) + jnp.log1p(jnp.exp(-jnp.abs(value)))


def sigmoid(value):
    return 1.0 / (1.0 + jnp.exp(-value))


def vmem_specs(count):
    return [pl.BlockSpec(memory_space=VMEM)] * count


def params(mib):
    return pltpu.CompilerParams(vmem_limit_bytes=mib * MIB)


def shape(dims, dtype=BF16):
    return jax.ShapeDtypeStruct(dims, dtype)


def start_chunks(chunks, most, weights_ref, held, sems):
    for chunk in range(most):
        @pl.when(chunk < chunks)
        def _():
            at = pl.ds(chunk * CHUNK, CHUNK)
            pltpu.make_async_copy(weights_ref.at[at], held.at[at], sems.at[chunk]).start()


def wait_chunk(chunk, weights_ref, held, sems):
    at = pl.ds(chunk * CHUNK, CHUNK)
    pltpu.make_async_copy(weights_ref.at[at], held.at[at], sems.at[chunk]).wait()


def prepare_kernel(chunks_ref, row_slot, weights_ref, degree_ref, turned_ref, held, turned, total, sems, out_sems):
    chunks = chunks_ref[0]
    most = held.shape[0] // CHUNK
    start_chunks(chunks, most, weights_ref, held, sems)
    total[...] = jnp.zeros_like(total)
    ones = jnp.ones((16, TS), BF16)

    def out_copy(chunk):
        at = pl.ds(chunk * CHUNK, CHUNK)
        return pltpu.make_async_copy(turned.at[at], turned_ref.at[at], out_sems.at[chunk])

    def step(chunk, carry):
        wait_chunk(chunk, weights_ref, held, sems)
        for lane in range(CHUNK):
            slot = chunk * CHUNK + lane
            tile = held[slot]
            sums = lax.dot_general(ones, tile, (((1,), (1,)), ((), ())), preferred_element_type=F32)
            at = pl.ds(row_slot[slot], 1)
            total[at, :] += sums[:1]
            turned[slot] = tile.T
        out_copy(chunk).start()
        return carry

    lax.fori_loop(0, chunks, step, 0)
    degree_ref[...] = total[:64]

    def finish(chunk, carry):
        out_copy(chunk).wait()
        return carry

    lax.fori_loop(0, chunks, finish, 0)


def prepare(chunks, row_slot, weights):
    slots = weights.shape[0]
    return pl.pallas_call(
        prepare_kernel,
        out_shape=(shape((64, TS), F32), shape(weights.shape)),
        in_specs=[pl.BlockSpec(memory_space=pltpu.SMEM)] * 2 + [pl.BlockSpec(memory_space=pl.ANY)],
        out_specs=(pl.BlockSpec(memory_space=VMEM), pl.BlockSpec(memory_space=pl.ANY)),
        scratch_shapes=[
            VMEM(weights.shape, BF16),
            VMEM(weights.shape, BF16),
            VMEM((72, TS), F32),
            pltpu.SemaphoreType.DMA((slots // CHUNK,)),
            pltpu.SemaphoreType.DMA((slots // CHUNK,)),
        ],
        compiler_params=params(24),
        cost_estimate=pl.CostEstimate(flops=slots * 2 * 16 * TS * TS, bytes_accessed=slots * TS * TS * 4, transcendentals=0),
        name="prepare",
    )(chunks, row_slot, weights)


def power_kernel(features_ref, out_ref):
    out_ref[...] = jnp.exp(EXPONENT * jnp.log(softplus(features_ref[...].astype(F32)))).astype(BF16)


def power(features):
    return pl.pallas_call(
        power_kernel, out_shape=shape(features.shape), in_specs=vmem_specs(1), out_specs=pl.BlockSpec(memory_space=VMEM), name="power"
    )(features)


def forward_kernel(chunks_ref, row_slot, col_slot, own_ref, other_ref, degree_ref, weights_ref, *rest):
    out_a, out_b = rest[:4], rest[4:8]
    held, panel, total, sems = rest[8:]
    chunks = chunks_ref[0]
    start_chunks(chunks, held.shape[0] // CHUNK, weights_ref, held, sems)
    panel[0:8] = own_ref[...]
    panel[8:16] = other_ref[...]

    def clear(at, carry):
        total[at] = jnp.zeros((TS, H), F32)
        return carry

    lax.fori_loop(0, 64, clear, 0)

    def step(chunk, carry):
        wait_chunk(chunk, weights_ref, held, sems)
        for lane in range(CHUNK):
            slot = chunk * CHUNK + lane
            at = row_slot[slot]
            total[at] += jnp.dot(held[slot], panel[col_slot[slot]], preferred_element_type=F32)
        return carry

    lax.fori_loop(0, chunks, step, 0)
    for dy in range(4):
        for dx in range(4):
            def put(dz, carry):
                value = total[dy * 16 + dx * 4 + dz].astype(BF16)
                out_a[dy][pl.ds((dx * 4 + dz) * TS, TS), :] = value[:, :HALF]
                out_b[dx][pl.ds((dy * 4 + dz) * TS, TS), :] = value[:, HALF:]
                return carry

            lax.fori_loop(0, 4, put, 0)
        degree = degree_ref[dy * 16 : dy * 16 + 16]
        high = degree.astype(BF16)
        out_a[dy][2048:2064, :] = high
        out_a[dy][2064:2080, :] = (degree - high.astype(F32)).astype(BF16)


def forward(chunks, row_slot, col_slot, own, other, degree, weights):
    slots = weights.shape[0]
    return pl.pallas_call(
        forward_kernel,
        out_shape=tuple([shape((2080, HALF))] * 4 + [shape((2048, HALF))] * 4),
        in_specs=[pl.BlockSpec(memory_space=pltpu.SMEM)] * 3 + vmem_specs(3) + [pl.BlockSpec(memory_space=pl.ANY)],
        out_specs=tuple(vmem_specs(8)),
        scratch_shapes=[
            VMEM(weights.shape, BF16),
            VMEM((16, TS, H), BF16),
            VMEM((65, TS, H), F32),
            pltpu.SemaphoreType.DMA((slots // CHUNK,)),
        ],
        compiler_params=params(40),
        cost_estimate=pl.CostEstimate(flops=slots * 2 * TS * TS * H, bytes_accessed=slots * TS * TS * 2, transcendentals=0),
        name="forward",
    )(chunks, row_slot, col_slot, own, other, degree, weights)


def sum_refs(refs, at):
    total = refs[0][at].astype(F32)
    for ref in refs[1:]:
        total = total + ref[at].astype(F32)
    return total


def split_degree(degree, rows):
    high = degree.astype(BF16).astype(F32)
    pieces = [high, degree - high]
    have = 2 * degree.shape[0]
    if have < rows:
        pieces.append(jnp.zeros((rows - have, degree.shape[1]), F32))
    return jnp.concatenate(pieces, axis=0).astype(BF16)


def fold_kernel(with_degree, *refs):
    parts, outs = refs[:4], refs[4:]
    for index, out in enumerate(outs):
        out[0:512, :] = sum_refs(parts, (slice(index * 512, index * 512 + 512), slice(None))).astype(BF16)
    if with_degree:
        tail = sum_refs(parts, (slice(2048, 2080), slice(None)))
        degree = tail[:16] + tail[16:]
        for index, out in enumerate(outs):
            out[512:528, :] = split_degree(degree[index * 4 : index * 4 + 4], 16)


def fold(parts, with_degree):
    rows = 528 if with_degree else 512
    return pl.pallas_call(
        lambda *refs: fold_kernel(with_degree, *refs),
        out_shape=tuple([shape((rows, HALF))] * 4),
        in_specs=vmem_specs(4),
        out_specs=tuple(vmem_specs(4)),
        compiler_params=params(8),
        name="fold",
    )(*parts)


def join_kernel(*refs):
    parts_a, parts_b, outs = refs[:4], refs[4:8], refs[8:]
    tail = sum_refs(parts_a, (slice(512, 528), slice(None)))
    degree = tail[0:4] + tail[4:8]
    high = degree.astype(BF16).astype(F32)
    low = degree - high
    for index, out in enumerate(outs):
        rows = (slice(index * TS, index * TS + TS), slice(None))
        out[0:TS, :HALF] = sum_refs(parts_a, rows).astype(BF16)
        out[0:TS, HALF:] = sum_refs(parts_b, rows).astype(BF16)
        out[TS : TS + 16, :HALF] = jnp.broadcast_to(high[index : index + 1], (16, HALF)).astype(BF16)
        out[TS : TS + 16, HALF:] = jnp.broadcast_to(low[index : index + 1], (16, HALF)).astype(BF16)


def join(parts_a, parts_b):
    return pl.pallas_call(
        join_kernel,
        out_shape=tuple([shape((TS + 16, H))] * 4),
        in_specs=vmem_specs(8),
        out_specs=tuple(vmem_specs(4)),
        compiler_params=params(8),
        name="join",
    )(*parts_a, *parts_b)


def terms_kernel(p0, p1, p2, p3, features_ref, cotangent_ref, first_ref, second_ref, scaled_ref, grad_ref, half_ref):
    parts = (p0, p1, p2, p3)
    neighbour = sum_refs(parts, (slice(0, TS), slice(None)))
    tail = sum_refs(parts, (slice(TS, TS + 16), slice(None)))
    degree = tail[0:1, :HALF] + tail[0:1, HALF:]
    column = 1.0 + jnp.broadcast_to(degree, (TS, HALF)).T
    denominator = jnp.concatenate([column, column], axis=1)
    as_float = features_ref[...].astype(F32)
    powered = jnp.exp(EXPONENT * jnp.log(softplus(as_float)))
    mean_pow = (powered + neighbour) / denominator
    aggregated = jnp.exp(jnp.log(mean_pow) / EXPONENT)
    mixed = (aggregated + as_float).astype(BF16)
    pre_act = jnp.dot(mixed, first_ref[...], preferred_element_type=F32)
    grad_act = lax.dot_general(cotangent_ref[...], second_ref[...], (((1,), (1,)), ((), ())), preferred_element_type=F32)
    gate = sigmoid(pre_act)
    grad_pre = (grad_act * gate * (1.0 + pre_act * (1.0 - gate))).astype(BF16)
    grad_mixed = lax.dot_general(grad_pre, first_ref[...], (((1,), (1,)), ((), ())), preferred_element_type=F32)
    scaled = grad_mixed * aggregated / (EXPONENT * mean_pow) / denominator
    scaled_ref[...] = scaled
    grad_ref[...] = grad_mixed
    half_ref[...] = scaled.astype(BF16)


def terms(parts, features, cotangent, first, second):
    return pl.pallas_call(
        terms_kernel,
        out_shape=(shape((TS, H), F32), shape((TS, H), F32), shape((TS, H))),
        in_specs=vmem_specs(8),
        out_specs=tuple(vmem_specs(3)),
        compiler_params=params(16),
        name="terms",
    )(*parts, features, cotangent, first, second)


def backward_kernel(chunks_ref, row_slot, col_slot, *rest):
    pieces, weights_ref, out_own, out_other = rest[:10], rest[10], rest[11], rest[12]
    held, source, total, sems, piece_sems = rest[13:]
    chunks = chunks_ref[0]
    low, high = pl.ds(0, HALF), pl.ds(HALF, HALF)
    whole, first, last = pl.ds(0, 4), pl.ds(0, 2), pl.ds(2, 2)
    targets = []
    for slab, part in ((0, whole), (1, whole), (2, first), (2, last), (3, whole)):
        targets.append(source.at[slab, part, :, :, low])
    for slab, part in ((0, whole), (1, whole), (2, first), (2, last), (3, whole)):
        targets.append(source.at[part, slab, :, :, high])
    copies = [pltpu.make_async_copy(piece, target, piece_sems.at[i]) for i, (piece, target) in enumerate(zip(pieces, targets))]
    for copy in copies:
        copy.start()
    start_chunks(chunks, held.shape[0] // CHUNK, weights_ref, held, sems)
    total[...] = jnp.zeros_like(total)
    for copy in copies:
        copy.wait()

    def step(chunk, carry):
        wait_chunk(chunk, weights_ref, held, sems)
        for lane in range(CHUNK):
            slot = chunk * CHUNK + lane
            at, row = col_slot[slot], row_slot[slot]
            tile = source[row // 16, row // 4 % 4, row % 4]
            total[at] += jnp.dot(held[slot], tile, preferred_element_type=F32)
        return carry

    lax.fori_loop(0, chunks, step, 0)
    out_own[...] = total[0:8].astype(BF16)
    out_other[...] = total[8:16].astype(BF16)


def backward(chunks, row_slot, col_slot, pieces, turned):
    slots = turned.shape[0]
    return pl.pallas_call(
        backward_kernel,
        out_shape=(shape((8, TS, H)), shape((8, TS, H))),
        in_specs=[pl.BlockSpec(memory_space=pltpu.SMEM)] * 3 + [pl.BlockSpec(memory_space=pl.ANY)] * 11,
        out_specs=tuple(vmem_specs(2)),
        scratch_shapes=[
            VMEM(turned.shape, BF16),
            VMEM((4, 4, 4, TS, H), BF16),
            VMEM((17, TS, H), F32),
            pltpu.SemaphoreType.DMA((slots // CHUNK,)),
            pltpu.SemaphoreType.DMA((10,)),
        ],
        compiler_params=params(32),
        cost_estimate=pl.CostEstimate(flops=slots * 2 * TS * TS * H, bytes_accessed=slots * TS * TS * 2, transcendentals=0),
        name="backward",
    )(chunks, row_slot, col_slot, *pieces, turned)


def fold_core_kernel(own_ref, got_ref, *outs):
    for index, out in enumerate(outs):
        at = slice(2 * index, 2 * index + 2)
        out[...] = (own_ref[at].astype(F32) + got_ref[at].astype(F32)).astype(BF16)


def fold_core(own, got):
    return pl.pallas_call(
        fold_core_kernel,
        out_shape=tuple([shape((2, TS, H))] * 4),
        in_specs=vmem_specs(2),
        out_specs=tuple(vmem_specs(4)),
        compiler_params=params(8),
        name="fold_core",
    )(own, got)


def fold_y_kernel(p0, p1, p2, p3, own_ref, other_ref):
    parts = (p0, p1, p2, p3)
    own_ref[...] = sum_refs(parts, 0)
    other_ref[...] = sum_refs(parts, 1).astype(BF16)


def fold_y(parts):
    return pl.pallas_call(
        fold_y_kernel,
        out_shape=(shape((TS, H), F32), shape((TS, H))),
        in_specs=vmem_specs(4),
        out_specs=tuple(vmem_specs(2)),
        compiler_params=params(8),
        name="fold_y",
    )(*parts)


def final_kernel(own_ref, got_ref, scaled_ref, grad_ref, features_ref, cotangent_ref, out_ref):
    as_float = features_ref[...].astype(F32)
    messages = softplus(as_float)
    powered = jnp.exp(EXPONENT * jnp.log(messages))
    back_sums = own_ref[...] + got_ref[...].astype(F32)
    grad_message = (scaled_ref[...] + back_sums) * (EXPONENT * powered / messages) * sigmoid(as_float)
    out_ref[...] = cotangent_ref[...].astype(F32) + grad_ref[...] + grad_message


def final(own, got, scaled, grad, features, cotangent):
    return pl.pallas_call(
        final_kernel,
        out_shape=shape((TS, H), F32),
        in_specs=vmem_specs(6),
        out_specs=pl.BlockSpec(memory_space=VMEM),
        compiler_params=params(8),
        name="final",
    )(own, got, scaled, grad, features, cotangent)


def direct(value, axis):
    return [value] + [shift(value, axis, step) for step in (1, 2, 3)]


def ring(value, axis):
    behind, ahead = shift(value, axis, 1), shift(value, axis, 3)
    return value, behind, shift(behind[:2], axis, 1), shift(ahead[2:], axis, 3), ahead


def spread(slabs, axis):
    return [slabs[0]] + [shift(slabs[step], axis, step) for step in (1, 2, 3)]


def local(features, cotangent, w_first, w_second, weights, tile_rows, tile_cols, tile_counts):
    slots = weights.shape[0]
    zh, core, zl, x, y = (lax.axis_index(axis) for axis in AXES)
    live = jnp.arange(slots, dtype=jnp.int32) < tile_counts[0]
    chunks = (tile_counts + CHUNK - 1) // CHUNK
    row_z, row_x, row_y = tile_rows // 16, tile_rows // 4 % 4, tile_rows % 4
    row_ahead = ((row_y - y) & 3) * 16 + ((row_x - x) & 3) * 4 + ((row_z - zl) & 3)
    row_behind = ((y - row_y) & 3) * 16 + ((x - row_x) & 3) * 4 + ((zl - row_z) & 3)
    col_h, col_core, col_y = tile_cols // 8, tile_cols // 4 % 2, tile_cols % 4
    col_base = (col_core ^ core) * 8 + (col_h ^ zh)
    col_ahead = col_base + ((col_y - y) & 3) * 2
    col_behind = col_base + ((y - col_y) & 3) * 2
    row_total = jnp.where(live, row_ahead, 64)
    col_total = jnp.where(live, col_ahead, 16)

    degree, turned = prepare(chunks, row_total, weights)
    powered = power(features)
    panel = jnp.stack([powered, swap(powered, "zh")])
    panel = jnp.concatenate(direct(panel, "y"), axis=0)
    slabs = forward(chunks, row_total, col_behind, panel, swap(panel, "core"), degree, weights)
    slabs_a, slabs_b = slabs[:4], slabs[4:]
    slabs_a, slabs_b = fold(spread(slabs_a, "y"), True), fold(spread(slabs_b, "x"), False)
    slabs = join(spread(slabs_a, "x"), spread(slabs_b, "y"))
    scaled, grad_mixed, scaled_half = terms(spread(slabs, "zl"), features, cotangent, w_first, w_second)

    rows = jnp.stack(direct(scaled_half, "zl"))
    rows_a, rows_b = rows[:, :, :HALF], rows[:, :, HALF:]
    rows_a = jnp.stack(direct(rows_a, "x"))
    rows_b = jnp.stack(direct(rows_b, "y"))
    pieces = (*ring(rows_a, "y"), *ring(rows_b, "x"))
    own, other = backward(chunks, row_behind, col_total, pieces, turned)
    slabs = fold_core(own, swap(other, "core"))
    own, other = fold_y(spread(slabs, "y"))
    return final(own, swap(other, "zh"), scaled, grad_mixed, features, cotangent)


def solution(mesh):
    split = Mesh(mesh.devices.reshape(2, 2, 4, 4, 4), AXES)
    placed = (P(AXES, None), P(AXES, None), P(), P(), P(AXES, None, None), P(AXES), P(AXES), P(AXES))
    return jax.shard_map(local, mesh=split, in_specs=placed, out_specs=P(AXES, None), check_vma=False)
```

```python
import jax
import jax.numpy as jnp
from jax import lax
from jax.experimental import pallas as pl
from jax.experimental.pallas import tpu as pltpu
from jax.sharding import Mesh
from jax.sharding import PartitionSpec as P

EXPONENT = 2.5
AXES = ("zh", "core", "zl", "x", "y")
TS = 128
H = 256
HALF = 128
CHUNK = 16
F32 = jnp.float32
BF16 = jnp.bfloat16
VMEM = pltpu.VMEM
MIB = 1 << 20


def shift(value, axis, step):
    return lax.ppermute(value, axis, [(i, (i + step) % 4) for i in range(4)])


def swap(value, axis):
    return lax.ppermute(value, axis, [(0, 1), (1, 0)])


def softplus(value):
    return jnp.maximum(value, 0.0) + jnp.log1p(jnp.exp(-jnp.abs(value)))


def sigmoid(value):
    return 1.0 / (1.0 + jnp.exp(-value))


def vmem_specs(count):
    return [pl.BlockSpec(memory_space=VMEM)] * count


def params(mib):
    return pltpu.CompilerParams(vmem_limit_bytes=mib * MIB)


def shape(dims, dtype=BF16):
    return jax.ShapeDtypeStruct(dims, dtype)


def start_chunks(chunks, most, weights_ref, held, sems):
    for chunk in range(most):
        @pl.when(chunk < chunks)
        def _():
            at = pl.ds(chunk * CHUNK, CHUNK)
            pltpu.make_async_copy(weights_ref.at[at], held.at[at], sems.at[chunk]).start()


def wait_chunk(chunk, weights_ref, held, sems):
    at = pl.ds(chunk * CHUNK, CHUNK)
    pltpu.make_async_copy(weights_ref.at[at], held.at[at], sems.at[chunk]).wait()


def power_kernel(features_ref, out_ref):
    out_ref[...] = jnp.exp(EXPONENT * jnp.log(softplus(features_ref[...].astype(F32)))).astype(BF16)


def power(features):
    return pl.pallas_call(
        power_kernel, out_shape=shape(features.shape), in_specs=vmem_specs(1), out_specs=pl.BlockSpec(memory_space=VMEM), name="power"
    )(features)


def forward_kernel(chunks_ref, row_slot, col_slot, p0, p1, p2, p3, weights_ref, *rest):
    out_a, out_b = rest[:5], rest[5:10]
    held, panel, total, degrees, sems = rest[10:]
    chunks = chunks_ref[0]
    start_chunks(chunks, held.shape[0] // CHUNK, weights_ref, held, sems)
    for index, part in enumerate((p0, p1, p2, p3)):
        panel[4 * index : 4 * index + 4] = part[...]

    def clear(at, carry):
        total[at] = jnp.zeros((TS, H), F32)
        return carry

    lax.fori_loop(0, 64, clear, 0)
    degrees[...] = jnp.zeros_like(degrees)
    ones = jnp.ones((16, TS), BF16)

    def step(chunk, carry):
        wait_chunk(chunk, weights_ref, held, sems)
        for lane in range(CHUNK):
            slot = chunk * CHUNK + lane
            at, tile = row_slot[slot], held[slot]
            total[at] += jnp.dot(tile, panel[col_slot[slot]], preferred_element_type=F32)
            sums = lax.dot_general(ones, tile, (((1,), (1,)), ((), ())), preferred_element_type=F32)
            degrees[pl.ds(at, 1), :] += sums[:1]
        return carry

    lax.fori_loop(0, chunks, step, 0)
    def target(outs, slab, part):
        if slab < 2:
            return outs[slab], part * 512
        if slab == 2:
            return outs[2 + part // 2], part % 2 * 512
        return outs[4], part * 512

    for dy in range(4):
        for dx in range(4):
            ref_a, base_a = target(out_a, dy, dx)
            ref_b, base_b = target(out_b, dx, dy)

            def put(dz, carry):
                value = total[dy * 16 + dx * 4 + dz].astype(BF16)
                ref_a[pl.ds(base_a + dz * TS, TS), :] = value[:, :HALF]
                ref_b[pl.ds(base_b + dz * TS, TS), :] = value[:, HALF:]
                return carry

            lax.fori_loop(0, 4, put, 0)
        degree = degrees[dy * 16 : dy * 16 + 16]
        high = degree.astype(BF16)
        ref = out_a[(0, 1, 2, 4)[dy]]
        base = ref.shape[0] - 32
        ref[base : base + 16, :] = high
        ref[base + 16 : base + 32, :] = (degree - high.astype(F32)).astype(BF16)


def forward(chunks, row_slot, col_slot, parts, weights):
    slots = weights.shape[0]
    return pl.pallas_call(
        forward_kernel,
        out_shape=tuple(shape((rows, HALF)) for rows in (2080, 2080, 1056, 1024, 2080, 2048, 2048, 1024, 1024, 2048)),
        in_specs=[pl.BlockSpec(memory_space=pltpu.SMEM)] * 3 + vmem_specs(4) + [pl.BlockSpec(memory_space=pltpu.HBM)],
        out_specs=tuple(vmem_specs(10)),
        scratch_shapes=[
            VMEM(weights.shape, BF16),
            VMEM((16, TS, H), BF16),
            VMEM((65, TS, H), F32),
            VMEM((72, TS), F32),
            pltpu.SemaphoreType.DMA((slots // CHUNK,)),
        ],
        compiler_params=params(40),
        cost_estimate=pl.CostEstimate(flops=slots * 2 * TS * TS * H, bytes_accessed=slots * TS * TS * 2, transcendentals=0),
        name="forward",
    )(chunks, row_slot, col_slot, *parts, weights)


def sum_refs(refs, at):
    total = refs[0][at].astype(F32)
    for ref in refs[1:]:
        total = total + ref[at].astype(F32)
    return total


def split_degree(degree, rows):
    high = degree.astype(BF16).astype(F32)
    pieces = [high, degree - high]
    have = 2 * degree.shape[0]
    if have < rows:
        pieces.append(jnp.zeros((rows - have, degree.shape[1]), F32))
    return jnp.concatenate(pieces, axis=0).astype(BF16)


def fold_kernel(with_degree, *refs):
    parts, outs = refs[:-4], refs[-4:]
    for index, out in enumerate(outs):
        out[0:512, :] = sum_refs(parts, (slice(index * 512, index * 512 + 512), slice(None))).astype(BF16)
    if with_degree:
        tail = sum_refs(parts, (slice(2048, 2080), slice(None)))
        degree = tail[:16] + tail[16:]
        for index, out in enumerate(outs):
            out[512:528, :] = split_degree(degree[index * 4 : index * 4 + 4], 16)


def fold(parts, with_degree):
    rows = 528 if with_degree else 512
    return pl.pallas_call(
        lambda *refs: fold_kernel(with_degree, *refs),
        out_shape=tuple([shape((rows, HALF))] * 4),
        in_specs=vmem_specs(len(parts)),
        out_specs=tuple(vmem_specs(4)),
        compiler_params=params(8),
        name="fold",
    )(*parts)


def relay_kernel(with_degree, behind_ref, ahead_ref, got_first, got_last, out_behind, out_ahead):
    first, last = (slice(0, 1024), slice(None)), (slice(1024, 2048), slice(None))
    out_behind[first] = sum_refs((behind_ref, got_first), first).astype(BF16)
    out_behind[last] = behind_ref[last]
    out_ahead[first] = ahead_ref[first]
    out_ahead[last] = (ahead_ref[last].astype(F32) + got_last[...].astype(F32)).astype(BF16)
    if with_degree:
        tail = behind_ref[2048:2080, :].astype(F32) + got_first[1024:1056, :].astype(F32)
        out_behind[2048:2080, :] = split_degree(tail[:16] + tail[16:], 32)
        out_ahead[2048:2080, :] = ahead_ref[2048:2080, :]


def relay(behind, ahead, got_first, got_last, with_degree):
    return pl.pallas_call(
        lambda *refs: relay_kernel(with_degree, *refs),
        out_shape=(shape(behind.shape), shape(ahead.shape)),
        in_specs=vmem_specs(4),
        out_specs=tuple(vmem_specs(2)),
        compiler_params=params(8),
        name="relay",
    )(behind, ahead, got_first, got_last)


def join_kernel(*refs):
    parts_a, parts_b, outs = refs[:4], refs[4:8], refs[8:]
    tail = sum_refs(parts_a, (slice(512, 528), slice(None)))
    degree = tail[0:4] + tail[4:8]
    high = degree.astype(BF16).astype(F32)
    low = degree - high
    for index, out in enumerate(outs):
        rows = (slice(index * TS, index * TS + TS), slice(None))
        out[0:TS, :HALF] = sum_refs(parts_a, rows).astype(BF16)
        out[0:TS, HALF:] = sum_refs(parts_b, rows).astype(BF16)
        out[TS : TS + 16, :HALF] = jnp.broadcast_to(high[index : index + 1], (16, HALF)).astype(BF16)
        out[TS : TS + 16, HALF:] = jnp.broadcast_to(low[index : index + 1], (16, HALF)).astype(BF16)


def join(parts_a, parts_b):
    return pl.pallas_call(
        join_kernel,
        out_shape=tuple([shape((TS + 16, H))] * 4),
        in_specs=vmem_specs(8),
        out_specs=tuple(vmem_specs(4)),
        compiler_params=params(8),
        name="join",
    )(*parts_a, *parts_b)


def terms_kernel(p0, p1, p2, p3, features_ref, cotangent_ref, first_ref, second_ref, scaled_ref, grad_ref, half_ref):
    parts = (p0, p1, p2, p3)
    neighbour = sum_refs(parts, (slice(0, TS), slice(None)))
    tail = sum_refs(parts, (slice(TS, TS + 16), slice(None)))
    degree = tail[0:1, :HALF] + tail[0:1, HALF:]
    column = 1.0 + jnp.broadcast_to(degree, (TS, HALF)).T
    denominator = jnp.concatenate([column, column], axis=1)
    as_float = features_ref[...].astype(F32)
    powered = jnp.exp(EXPONENT * jnp.log(softplus(as_float)))
    mean_pow = (powered + neighbour) / denominator
    aggregated = jnp.exp(jnp.log(mean_pow) / EXPONENT)
    mixed = (aggregated + as_float).astype(BF16)
    pre_act = jnp.dot(mixed, first_ref[...], preferred_element_type=F32)
    grad_act = lax.dot_general(cotangent_ref[...], second_ref[...], (((1,), (1,)), ((), ())), preferred_element_type=F32)
    gate = sigmoid(pre_act)
    grad_pre = (grad_act * gate * (1.0 + pre_act * (1.0 - gate))).astype(BF16)
    grad_mixed = lax.dot_general(grad_pre, first_ref[...], (((1,), (1,)), ((), ())), preferred_element_type=F32)
    scaled = grad_mixed * aggregated / (EXPONENT * mean_pow) / denominator
    scaled_ref[...] = scaled
    grad_ref[...] = grad_mixed
    half_ref[...] = scaled.astype(BF16)


def terms(parts, features, cotangent, first, second):
    return pl.pallas_call(
        terms_kernel,
        out_shape=(shape((TS, H), F32), shape((TS, H), F32), shape((TS, H))),
        in_specs=vmem_specs(8),
        out_specs=tuple(vmem_specs(3)),
        compiler_params=params(16),
        name="terms",
    )(*parts, features, cotangent, first, second)


def backward_kernel(chunks_ref, row_slot, col_slot, *rest):
    pieces, weights_ref, outs = rest[:10], rest[10], rest[11:15]
    held, source, total, sems, piece_sems = rest[15:]
    chunks = chunks_ref[0]
    low, high = pl.ds(0, HALF), pl.ds(HALF, HALF)
    whole, first, last = pl.ds(0, 4), pl.ds(0, 2), pl.ds(2, 2)
    targets = []
    for slab, part in ((0, whole), (1, whole), (2, first), (2, last), (3, whole)):
        targets.append(source.at[slab, part, :, :, low])
    for slab, part in ((0, whole), (1, whole), (2, first), (2, last), (3, whole)):
        targets.append(source.at[part, slab, :, :, high])
    copies = [pltpu.make_async_copy(piece, target, piece_sems.at[i]) for i, (piece, target) in enumerate(zip(pieces, targets))]
    for copy in copies:
        copy.start()
    start_chunks(chunks, held.shape[0] // CHUNK, weights_ref, held, sems)
    total[...] = jnp.zeros_like(total)
    for copy in copies:
        copy.wait()

    def step(chunk, carry):
        wait_chunk(chunk, weights_ref, held, sems)
        for lane in range(CHUNK):
            slot = chunk * CHUNK + lane
            at, row = col_slot[slot], row_slot[slot]
            tile = source[row // 16, row // 4 % 4, row % 4]
            total[at] += lax.dot_general(held[slot], tile, (((0,), (0,)), ((), ())), preferred_element_type=F32)
        return carry

    lax.fori_loop(0, chunks, step, 0)
    for index, out in enumerate(outs):
        out[...] = total[4 * index : 4 * index + 4].astype(BF16)


def backward(chunks, row_slot, col_slot, pieces, weights):
    slots = weights.shape[0]
    return pl.pallas_call(
        backward_kernel,
        out_shape=tuple([shape((4, TS, H))] * 4),
        in_specs=[pl.BlockSpec(memory_space=pltpu.SMEM)] * 3 + [pl.BlockSpec(memory_space=pl.ANY)] * 10 + [pl.BlockSpec(memory_space=pltpu.HBM)],
        out_specs=tuple(vmem_specs(4)),
        scratch_shapes=[
            VMEM(weights.shape, BF16),
            VMEM((4, 4, 4, TS, H), BF16),
            VMEM((17, TS, H), F32),
            pltpu.SemaphoreType.DMA((slots // CHUNK,)),
            pltpu.SemaphoreType.DMA((10,)),
        ],
        compiler_params=params(32),
        cost_estimate=pl.CostEstimate(flops=slots * 2 * TS * TS * H, bytes_accessed=slots * TS * TS * 2, transcendentals=0),
        name="backward",
    )(chunks, row_slot, col_slot, *pieces, weights)


def fold_core_kernel(own_ref, got_ref, *outs):
    for index, out in enumerate(outs):
        out[...] = (own_ref[index].astype(F32) + got_ref[index].astype(F32)).astype(BF16)


def fold_core(own, got):
    return pl.pallas_call(
        fold_core_kernel,
        out_shape=tuple([shape((TS, H))] * 4),
        in_specs=vmem_specs(2),
        out_specs=tuple(vmem_specs(4)),
        compiler_params=params(8),
        name="fold_core",
    )(own, got)


def fold_y_kernel(p0, p1, p2, p3, out_ref):
    out_ref[...] = sum_refs((p0, p1, p2, p3), slice(None)).astype(out_ref.dtype)


def fold_y(parts, dtype):
    return pl.pallas_call(
        fold_y_kernel,
        out_shape=shape((TS, H), dtype),
        in_specs=vmem_specs(4),
        out_specs=pl.BlockSpec(memory_space=VMEM),
        compiler_params=params(8),
        name="fold_y",
    )(*parts)


def final_kernel(p0, p1, p2, p3, got_ref, scaled_ref, grad_ref, features_ref, cotangent_ref, out_ref):
    as_float = features_ref[...].astype(F32)
    messages = softplus(as_float)
    powered = jnp.exp(EXPONENT * jnp.log(messages))
    back_sums = sum_refs((p0, p1, p2, p3, got_ref), slice(None))
    grad_message = (scaled_ref[...] + back_sums) * (EXPONENT * powered / messages) * sigmoid(as_float)
    out_ref[...] = cotangent_ref[...].astype(F32) + grad_ref[...] + grad_message


def final(parts, got, scaled, grad, features, cotangent):
    return pl.pallas_call(
        final_kernel,
        out_shape=shape((TS, H), F32),
        in_specs=vmem_specs(9),
        out_specs=pl.BlockSpec(memory_space=VMEM),
        compiler_params=params(8),
        name="final",
    )(*parts, got, scaled, grad, features, cotangent)


def direct(value, axis):
    return [value] + [shift(value, axis, step) for step in (1, 2, 3)]


def ring(value, axis):
    behind, ahead = shift(value, axis, 1), shift(value, axis, 3)
    return value, behind, shift(behind[:2], axis, 1), shift(ahead[2:], axis, 3), ahead


def ring_sums(slabs, axis, with_degree):
    own, behind, first, last, ahead = slabs
    got_first, got_last = shift(first, axis, 1), shift(last, axis, 3)
    behind, ahead = relay(behind, ahead, got_first, got_last, with_degree)
    return own, shift(behind, axis, 1), shift(ahead, axis, 3)


def spread(slabs, axis):
    return [slabs[0]] + [shift(slabs[step], axis, step) for step in (1, 2, 3)]


def local(features, cotangent, w_first, w_second, weights, tile_rows, tile_cols, tile_counts):
    slots = weights.shape[0]
    zh, core, zl, x, y = (lax.axis_index(axis) for axis in AXES)
    live = jnp.arange(slots, dtype=jnp.int32) < tile_counts[0]
    chunks = (tile_counts + CHUNK - 1) // CHUNK
    row_z, row_x, row_y = tile_rows // 16, tile_rows // 4 % 4, tile_rows % 4
    row_ahead = ((row_y - y) & 3) * 16 + ((row_x - x) & 3) * 4 + ((row_z - zl) & 3)
    row_behind = ((y - row_y) & 3) * 16 + ((x - row_x) & 3) * 4 + ((zl - row_z) & 3)
    col_h, col_core, col_y = tile_cols // 8, tile_cols // 4 % 2, tile_cols % 4
    col_base = (col_core ^ core) * 8 + (col_h ^ zh) * 4
    col_ahead = col_base + ((col_y - y) & 3)
    col_behind = col_base + ((y - col_y) & 3)
    row_total = jnp.where(live, row_ahead, 64)
    col_total = jnp.where(live, col_ahead, 16)

    powered = power(features)
    far = swap(powered, "zh")
    near = jnp.stack(direct(powered, "y"))
    near_other = swap(near, "core")
    far = jnp.stack(direct(far, "y"))
    weights = pltpu.with_memory_space_constraint(weights, pltpu.HBM)
    panels = (near, far, near_other, swap(far, "core"))
    slabs = forward(chunks, row_total, col_behind, panels, weights)
    slabs_a, slabs_b = fold(ring_sums(slabs[:5], "y", True), True), fold(ring_sums(slabs[5:], "x", False), False)
    slabs = join(spread(slabs_a, "x"), spread(slabs_b, "y"))
    scaled, grad_mixed, scaled_half = terms(spread(slabs, "zl"), features, cotangent, w_first, w_second)

    rows = jnp.stack(direct(scaled_half, "zl"))
    rows_a, rows_b = rows[:, :, :HALF], rows[:, :, HALF:]
    rows_a = jnp.stack(direct(rows_a, "x"))
    rows_b = jnp.stack(direct(rows_b, "y"))
    pieces = (*ring(rows_a, "y"), *ring(rows_b, "x"))
    own_near, own_far, other_near, other_far = backward(chunks, row_behind, col_total, pieces, weights)
    far = fold_y(spread(fold_core(own_far, swap(other_far, "core")), "y"), BF16)
    near = spread(fold_core(own_near, swap(other_near, "core")), "y")
    return final(near, swap(far, "zh"), scaled, grad_mixed, features, cotangent)


def solution(mesh):
    split = Mesh(mesh.devices.reshape(2, 2, 4, 4, 4), AXES)
    placed = (P(AXES, None), P(AXES, None), P(), P(), P(AXES, None, None), P(AXES), P(AXES), P(AXES))
    return jax.shard_map(local, mesh=split, in_specs=placed, out_specs=P(AXES, None), check_vma=False)
```

```python
import jax
import jax.numpy as jnp
from jax import lax
from jax.experimental import pallas as pl
from jax.experimental.pallas import tpu as pltpu
from jax.sharding import Mesh
from jax.sharding import PartitionSpec as P

EXPONENT = 2.5
AXES = ("zh", "core", "zl", "x", "y")
TS = 128
H = 256
HALF = 128
CHUNK = 32
STEP = 32
F32 = jnp.float32
BF16 = jnp.bfloat16
VMEM = pltpu.VMEM
MIB = 1 << 20


def shift(value, axis, step):
    return lax.ppermute(value, axis, [(i, (i + step) % 4) for i in range(4)])


def swap(value, axis):
    return lax.ppermute(value, axis, [(0, 1), (1, 0)])


def softplus(value):
    return jnp.maximum(value, 0.0) + jnp.log1p(jnp.exp(-jnp.abs(value)))


def sigmoid(value):
    return 1.0 / (1.0 + jnp.exp(-value))


def vmem_specs(count):
    return [pl.BlockSpec(memory_space=VMEM)] * count


def params(mib):
    return pltpu.CompilerParams(vmem_limit_bytes=mib * MIB)


def shape(dims, dtype=BF16):
    return jax.ShapeDtypeStruct(dims, dtype)


def start_chunks(chunks, most, weights_ref, held, sems):
    for chunk in range(most):
        @pl.when(chunk < chunks)
        def _():
            at = pl.ds(chunk * CHUNK, CHUNK)
            pltpu.make_async_copy(weights_ref.at[at], held.at[at], sems.at[chunk]).start()


def wait_chunk(chunk, weights_ref, held, sems):
    at = pl.ds(chunk * CHUNK, CHUNK)
    pltpu.make_async_copy(weights_ref.at[at], held.at[at], sems.at[chunk]).wait()


def degree_kernel(chunks_ref, row_slot, weights_ref, degree_ref, held, total, sems):
    chunks = chunks_ref[0]
    start_chunks(chunks, held.shape[0] // CHUNK, weights_ref, held, sems)
    total[...] = jnp.zeros_like(total)
    ones = jnp.ones((16, TS), BF16)

    def step(chunk, carry):
        wait_chunk(chunk, weights_ref, held, sems)
        tiles = held[pl.ds(chunk * CHUNK, CHUNK)].reshape(CHUNK * TS, TS)
        sums = lax.dot_general(ones, tiles, (((1,), (1,)), ((), ())), preferred_element_type=F32)
        for lane in range(CHUNK):
            at = pl.ds(row_slot[chunk * CHUNK + lane], 1)
            total[at, :] += sums[:1, lane * TS : lane * TS + TS]
        return carry

    lax.fori_loop(0, chunks, step, 0)
    degree_ref[...] = total[:64]


def degrees(chunks, row_slot, weights):
    slots = weights.shape[0]
    return pl.pallas_call(
        degree_kernel,
        out_shape=shape((64, TS), F32),
        in_specs=[pl.BlockSpec(memory_space=pltpu.SMEM)] * 2 + [pl.BlockSpec(memory_space=pltpu.HBM)],
        out_specs=pl.BlockSpec(memory_space=VMEM),
        scratch_shapes=[
            VMEM(weights.shape, BF16),
            VMEM((72, TS), F32),
            pltpu.SemaphoreType.DMA((slots // CHUNK,)),
        ],
        compiler_params=params(16),
        cost_estimate=pl.CostEstimate(flops=slots * 2 * 16 * TS * TS, bytes_accessed=slots * TS * TS * 2, transcendentals=0),
        name="degrees",
    )(chunks, row_slot, weights)


def power_kernel(own_ref, far_ref, out_ref):
    for index, ref in enumerate((own_ref, far_ref)):
        out_ref[index] = jnp.exp(EXPONENT * jnp.log(softplus(ref[...].astype(F32)))).astype(BF16)


def power(own, far):
    return pl.pallas_call(
        power_kernel,
        out_shape=shape((2, *own.shape)),
        in_specs=vmem_specs(2),
        out_specs=pl.BlockSpec(memory_space=VMEM),
        compiler_params=params(8),
        name="power",
    )(own, far)


def stack_kernel(*refs):
    for index, ref in enumerate(refs[:-1]):
        def body(at, carry, index=index, ref=ref):
            refs[-1][index, at] = ref[at]
            return carry

        lax.fori_loop(0, ref.shape[0], body, 0)


def stack(parts):
    return pl.pallas_call(
        stack_kernel,
        out_shape=shape((len(parts), *parts[0].shape)),
        in_specs=vmem_specs(len(parts)),
        out_specs=pl.BlockSpec(memory_space=VMEM),
        compiler_params=params(8),
        name="stack",
    )(*parts)


def halves_kernel(*refs):
    for index, ref in enumerate(refs[:-2]):
        refs[-2][index] = ref[:, :HALF]
        refs[-1][index] = ref[:, HALF:]


def halves(parts):
    return pl.pallas_call(
        halves_kernel,
        out_shape=(shape((len(parts), TS, HALF)), shape((len(parts), TS, HALF))),
        in_specs=vmem_specs(len(parts)),
        out_specs=tuple(vmem_specs(2)),
        compiler_params=params(8),
        name="halves",
    )(*parts)


def forward_kernel(chunks_ref, row_slot, col_slot, *rest):
    pieces, degree_ref, weights_ref, rest = rest[:2], rest[2], rest[3], rest[4:]
    out_a, out_b = rest[:5], rest[5:10]
    held, panel, total, sems = rest[10:]
    chunks = chunks_ref[0]
    start_chunks(chunks, held.shape[0] // CHUNK, weights_ref, held, sems)
    for index, piece in enumerate(pieces):
        def copy(at, carry, index=index, piece=piece):
            for part in range(2):
                panel[index * 8 + at * 2 + part] = piece[at, part]
            return carry

        lax.fori_loop(0, 4, copy, 0)

    def clear(at, carry):
        total[at] = jnp.zeros((TS, H), F32)
        return carry

    lax.fori_loop(0, 64, clear, 0)

    def step(chunk, carry):
        wait_chunk(chunk, weights_ref, held, sems)
        def some(part, carry):
            for lane in range(STEP):
                slot = chunk * CHUNK + part * STEP + lane
                at = row_slot[slot]
                total[at] += jnp.dot(held[slot], panel[col_slot[slot]], preferred_element_type=F32)
            return carry

        return lax.fori_loop(0, CHUNK // STEP, some, carry)

    lax.fori_loop(0, chunks, step, 0)
    def target(outs, slab, part):
        if slab < 2:
            return outs[slab], part * 512
        if slab == 2:
            return outs[2 + part // 2], part % 2 * 512
        return outs[4], part * 512

    for dy in range(4):
        for dx in range(4):
            ref_a, base_a = target(out_a, dy, dx)
            ref_b, base_b = target(out_b, dx, dy)

            def put(dz, carry):
                value = total[dy * 16 + dx * 4 + dz].astype(BF16)
                ref_a[pl.ds(base_a + dz * TS, TS), :] = value[:, :HALF]
                ref_b[pl.ds(base_b + dz * TS, TS), :] = value[:, HALF:]
                return carry

            lax.fori_loop(0, 4, put, 0)
        degree = degree_ref[dy * 16 : dy * 16 + 16]
        high = degree.astype(BF16)
        ref = out_a[(0, 1, 2, 4)[dy]]
        base = ref.shape[0] - 32
        ref[base : base + 16, :] = high
        ref[base + 16 : base + 32, :] = (degree - high.astype(F32)).astype(BF16)


def forward(chunks, row_slot, col_slot, parts, degree, weights):
    slots = weights.shape[0]
    return pl.pallas_call(
        forward_kernel,
        out_shape=tuple(shape((rows, HALF)) for rows in (2080, 2080, 1056, 1024, 2080, 2048, 2048, 1024, 1024, 2048)),
        in_specs=[pl.BlockSpec(memory_space=pltpu.SMEM)] * 3 + vmem_specs(3) + [pl.BlockSpec(memory_space=pltpu.HBM)],
        out_specs=tuple(vmem_specs(10)),
        scratch_shapes=[
            VMEM(weights.shape, BF16),
            VMEM((16, TS, H), BF16),
            VMEM((65, TS, H), F32),
            pltpu.SemaphoreType.DMA((slots // CHUNK,)),
        ],
        compiler_params=params(40),
        cost_estimate=pl.CostEstimate(flops=slots * 2 * TS * TS * H, bytes_accessed=slots * TS * TS * 2, transcendentals=0),
        name="forward",
    )(chunks, row_slot, col_slot, *parts, degree, weights)


def blocks(count, body):
    def step(index, carry):
        body(pl.ds(pl.multiple_of(index * TS, TS), TS))
        return carry

    lax.fori_loop(0, count, step, 0)


def sum_refs(refs, at):
    total = refs[0][at].astype(F32)
    for ref in refs[1:]:
        total = total + ref[at].astype(F32)
    return total


def split_degree(degree, rows):
    high = degree.astype(BF16).astype(F32)
    pieces = [high, degree - high]
    have = 2 * degree.shape[0]
    if have < rows:
        pieces.append(jnp.zeros((rows - have, degree.shape[1]), F32))
    return jnp.concatenate(pieces, axis=0).astype(BF16)


def fold_kernel(with_degree, *refs):
    parts, outs = refs[:-4], refs[-4:]
    for index, out in enumerate(outs):
        def body(rows, out=out, index=index):
            out[rows, :] = sum_refs(parts, (pl.ds(rows.start + index * 512, TS), slice(None))).astype(BF16)

        blocks(4, body)
    if with_degree:
        tail = sum_refs(parts, (slice(2048, 2080), slice(None)))
        degree = tail[:16] + tail[16:]
        for index, out in enumerate(outs):
            out[512:528, :] = split_degree(degree[index * 4 : index * 4 + 4], 16)


def fold(parts, with_degree):
    rows = 528 if with_degree else 512
    return pl.pallas_call(
        lambda *refs: fold_kernel(with_degree, *refs),
        out_shape=tuple([shape((rows, HALF))] * 4),
        in_specs=vmem_specs(len(parts)),
        out_specs=tuple(vmem_specs(4)),
        compiler_params=params(8),
        name="fold",
    )(*parts)


def relay_kernel(with_degree, behind_ref, ahead_ref, got_first, got_last, out_behind, out_ahead):
    def body(rows):
        later = pl.ds(rows.start + 1024, TS)
        out_behind[rows, :] = sum_refs((behind_ref, got_first), (rows, slice(None))).astype(BF16)
        out_behind[later, :] = behind_ref[later, :]
        out_ahead[rows, :] = ahead_ref[rows, :]
        out_ahead[later, :] = (ahead_ref[later, :].astype(F32) + got_last[rows, :].astype(F32)).astype(BF16)

    blocks(8, body)
    if with_degree:
        tail = behind_ref[2048:2080, :].astype(F32) + got_first[1024:1056, :].astype(F32)
        out_behind[2048:2080, :] = split_degree(tail[:16] + tail[16:], 32)
        out_ahead[2048:2080, :] = ahead_ref[2048:2080, :]


def relay(behind, ahead, got_first, got_last, with_degree):
    return pl.pallas_call(
        lambda *refs: relay_kernel(with_degree, *refs),
        out_shape=(shape(behind.shape), shape(ahead.shape)),
        in_specs=vmem_specs(4),
        out_specs=tuple(vmem_specs(2)),
        compiler_params=params(8),
        name="relay",
    )(behind, ahead, got_first, got_last)


def add_kernel(p0, p1, p2, p3, out_ref):
    def body(rows):
        out_ref[rows, :] = sum_refs((p0, p1, p2, p3), (rows, slice(None)))

    blocks(4, body)


def add(parts):
    return pl.pallas_call(
        add_kernel,
        out_shape=shape(parts[0].shape, F32),
        in_specs=vmem_specs(4),
        out_specs=pl.BlockSpec(memory_space=VMEM),
        compiler_params=params(8),
        name="add",
    )(*parts)


def join_kernel(*refs):
    parts_a, sums_b, outs = refs[:4], refs[4], refs[5:]
    tail = sum_refs(parts_a, (slice(512, 528), slice(None)))
    degree = tail[0:4] + tail[4:8]
    high = degree.astype(BF16).astype(F32)
    low = degree - high
    for index, out in enumerate(outs):
        rows = (slice(index * TS, index * TS + TS), slice(None))
        out[0:TS, :HALF] = sum_refs(parts_a, rows).astype(BF16)
        out[0:TS, HALF:] = sums_b[rows].astype(BF16)
        out[TS : TS + 16, :HALF] = jnp.broadcast_to(high[index : index + 1], (16, HALF)).astype(BF16)
        out[TS : TS + 16, HALF:] = jnp.broadcast_to(low[index : index + 1], (16, HALF)).astype(BF16)


def join(parts_a, sums_b):
    return pl.pallas_call(
        join_kernel,
        out_shape=tuple([shape((TS + 16, H))] * 4),
        in_specs=vmem_specs(5),
        out_specs=tuple(vmem_specs(4)),
        compiler_params=params(8),
        name="join",
    )(*parts_a, sums_b)


def terms_kernel(p0, p1, p2, p3, features_ref, cotangent_ref, first_ref, second_ref, scaled_ref, grad_ref, half_ref):
    parts = (p0, p1, p2, p3)
    neighbour = sum_refs(parts, (slice(0, TS), slice(None)))
    tail = sum_refs(parts, (slice(TS, TS + 16), slice(None)))
    degree = tail[0:1, :HALF] + tail[0:1, HALF:]
    column = 1.0 + jnp.broadcast_to(degree, (TS, HALF)).T
    denominator = jnp.concatenate([column, column], axis=1)
    as_float = features_ref[...].astype(F32)
    powered = jnp.exp(EXPONENT * jnp.log(softplus(as_float)))
    mean_pow = (powered + neighbour) / denominator
    aggregated = jnp.exp(jnp.log(mean_pow) / EXPONENT)
    mixed = (aggregated + as_float).astype(BF16)
    pre_act = jnp.dot(mixed, first_ref[...], preferred_element_type=F32)
    grad_act = lax.dot_general(cotangent_ref[...], second_ref[...], (((1,), (1,)), ((), ())), preferred_element_type=F32)
    gate = sigmoid(pre_act)
    grad_pre = (grad_act * gate * (1.0 + pre_act * (1.0 - gate))).astype(BF16)
    grad_mixed = lax.dot_general(grad_pre, first_ref[...], (((1,), (1,)), ((), ())), preferred_element_type=F32)
    scaled = grad_mixed * aggregated / (EXPONENT * mean_pow) / denominator
    scaled_ref[...] = scaled
    grad_ref[...] = grad_mixed
    half_ref[...] = scaled.astype(BF16)


def terms(parts, features, cotangent, first, second):
    return pl.pallas_call(
        terms_kernel,
        out_shape=(shape((TS, H), F32), shape((TS, H), F32), shape((TS, H))),
        in_specs=vmem_specs(8),
        out_specs=tuple(vmem_specs(3)),
        compiler_params=params(16),
        name="terms",
    )(*parts, features, cotangent, first, second)


def backward_kernel(chunks_ref, row_slot, col_slot, *rest):
    pieces, weights_ref, outs = rest[:10], rest[10], rest[11:13]
    held, source, total, sems, piece_sems = rest[13:]
    chunks = chunks_ref[0]
    low, high = pl.ds(0, HALF), pl.ds(HALF, HALF)
    whole, first, last = pl.ds(0, 4), pl.ds(0, 2), pl.ds(2, 2)
    targets = []
    for slab, part in ((0, whole), (1, whole), (2, first), (2, last), (3, whole)):
        targets.append(source.at[slab, part, :, :, low])
    for slab, part in ((0, whole), (1, whole), (2, first), (2, last), (3, whole)):
        targets.append(source.at[part, slab, :, :, high])
    copies = [pltpu.make_async_copy(piece, target, piece_sems.at[i]) for i, (piece, target) in enumerate(zip(pieces, targets))]
    for copy in copies:
        copy.start()
    start_chunks(chunks, held.shape[0] // CHUNK, weights_ref, held, sems)

    def clear(at, carry):
        total[at] = jnp.zeros((TS, H), F32)
        return carry

    lax.fori_loop(0, 16, clear, 0)
    for copy in copies:
        copy.wait()

    def step(chunk, carry):
        wait_chunk(chunk, weights_ref, held, sems)
        def some(part, carry):
            for lane in range(STEP):
                slot = chunk * CHUNK + part * STEP + lane
                at, row = col_slot[slot], row_slot[slot]
                tile = source[row // 16, row // 4 % 4, row % 4]
                total[at] += lax.dot_general(held[slot], tile, (((0,), (0,)), ((), ())), preferred_element_type=F32)
            return carry

        return lax.fori_loop(0, CHUNK // STEP, some, carry)

    lax.fori_loop(0, chunks, step, 0)
    for index, out in enumerate(outs):
        def put(at, carry, out=out, index=index):
            out[at] = total[8 * index + at].astype(BF16)
            return carry

        lax.fori_loop(0, 8, put, 0)


def backward(chunks, row_slot, col_slot, pieces, weights):
    slots = weights.shape[0]
    return pl.pallas_call(
        backward_kernel,
        out_shape=tuple([shape((8, TS, H))] * 2),
        in_specs=[pl.BlockSpec(memory_space=pltpu.SMEM)] * 3 + [pl.BlockSpec(memory_space=pl.ANY)] * 10 + [pl.BlockSpec(memory_space=pltpu.HBM)],
        out_specs=tuple(vmem_specs(2)),
        scratch_shapes=[
            VMEM(weights.shape, BF16),
            VMEM((4, 4, 4, TS, H), BF16),
            VMEM((17, TS, H), F32),
            pltpu.SemaphoreType.DMA((slots // CHUNK,)),
            pltpu.SemaphoreType.DMA((10,)),
        ],
        compiler_params=params(32),
        cost_estimate=pl.CostEstimate(flops=slots * 2 * TS * TS * H, bytes_accessed=slots * TS * TS * 2, transcendentals=0),
        name="backward",
    )(chunks, row_slot, col_slot, *pieces, weights)


def fold_core_kernel(own_ref, got_ref, *outs):
    for index, out in enumerate(outs):
        for part in range(2):
            at = 2 * index + part
            out[part] = (own_ref[at].astype(F32) + got_ref[at].astype(F32)).astype(BF16)


def fold_core(own, got):
    return pl.pallas_call(
        fold_core_kernel,
        out_shape=tuple([shape((2, TS, H))] * 4),
        in_specs=vmem_specs(2),
        out_specs=tuple(vmem_specs(4)),
        compiler_params=params(8),
        name="fold_core",
    )(own, got)


def fold_y_kernel(p0, p1, p2, p3, own_ref, far_ref):
    parts = (p0, p1, p2, p3)
    own_ref[...] = sum_refs(parts, 0)
    far_ref[...] = sum_refs(parts, 1).astype(BF16)


def fold_y(parts):
    return pl.pallas_call(
        fold_y_kernel,
        out_shape=(shape((TS, H), F32), shape((TS, H))),
        in_specs=vmem_specs(4),
        out_specs=tuple(vmem_specs(2)),
        compiler_params=params(8),
        name="fold_y",
    )(*parts)


def final_kernel(own_ref, got_ref, scaled_ref, grad_ref, features_ref, cotangent_ref, out_ref):
    as_float = features_ref[...].astype(F32)
    messages = softplus(as_float)
    powered = jnp.exp(EXPONENT * jnp.log(messages))
    back_sums = own_ref[...] + got_ref[...].astype(F32)
    grad_message = (scaled_ref[...] + back_sums) * (EXPONENT * powered / messages) * sigmoid(as_float)
    out_ref[...] = cotangent_ref[...].astype(F32) + grad_ref[...] + grad_message


def final(own, got, scaled, grad, features, cotangent):
    return pl.pallas_call(
        final_kernel,
        out_shape=shape((TS, H), F32),
        in_specs=vmem_specs(6),
        out_specs=pl.BlockSpec(memory_space=VMEM),
        compiler_params=params(8),
        name="final",
    )(own, got, scaled, grad, features, cotangent)


def direct(value, axis):
    return [value] + [shift(value, axis, step) for step in (1, 2, 3)]


def ring(value, axis):
    behind, ahead = shift(value, axis, 1), shift(value, axis, 3)
    return value, behind, shift(behind[:2], axis, 1), shift(ahead[2:], axis, 3), ahead


def ring_sums(slabs, axis, with_degree):
    own, behind, first, last, ahead = slabs
    got_first, got_last = shift(first, axis, 1), shift(last, axis, 3)
    behind, ahead = relay(behind, ahead, got_first, got_last, with_degree)
    return own, shift(behind, axis, 1), shift(ahead, axis, 3)


def spread(slabs, axis):
    return [slabs[0]] + [shift(slabs[step], axis, step) for step in (1, 2, 3)]


def local(features, cotangent, w_first, w_second, weights, tile_rows, tile_cols, tile_counts):
    slots = weights.shape[0]
    zh, core, zl, x, y = (lax.axis_index(axis) for axis in AXES)
    live = jnp.arange(slots, dtype=jnp.int32) < tile_counts[0]
    chunks = (tile_counts + CHUNK - 1) // CHUNK
    row_z, row_x, row_y = tile_rows // 16, tile_rows // 4 % 4, tile_rows % 4
    row_ahead = ((row_y - y) & 3) * 16 + ((row_x - x) & 3) * 4 + ((row_z - zl) & 3)
    row_behind = ((y - row_y) & 3) * 16 + ((x - row_x) & 3) * 4 + ((zl - row_z) & 3)
    col_h, col_core, col_y = tile_cols // 8, tile_cols // 4 % 2, tile_cols % 4
    col_base = (col_core ^ core) * 8 + (col_h ^ zh)
    row_total = jnp.where(live, row_ahead, 64)
    col_panel = col_base + ((y - col_y) & 3) * 2
    col_total = jnp.where(live, (col_core ^ core) * 8 + ((col_y - y) & 3) * 2 + (col_h ^ zh), 16)
    weights = pltpu.with_memory_space_constraint(weights, pltpu.HBM)

    far = swap(features, "zh")
    degree = degrees(chunks, row_total, weights)
    far, degree, col_panel = lax.optimization_barrier((far, degree, col_panel))
    panels = stack(direct(power(features, far), "y"))
    slabs = forward(chunks, row_total, col_panel, (panels, swap(panels, "core")), degree, weights)
    slabs_a, slabs_b = fold(ring_sums(slabs[:5], "y", True), True), fold(ring_sums(slabs[5:], "x", False), False)
    slabs = join(spread(slabs_a, "x"), add(spread(slabs_b, "y")))
    scaled, grad_mixed, scaled_half = terms(spread(slabs, "zl"), features, cotangent, w_first, w_second)

    rows_a, rows_b = halves(direct(scaled_half, "zl"))
    rows_a = stack(direct(rows_a, "x"))
    rows_b = stack(direct(rows_b, "y"))
    pieces = (*ring(rows_a, "y"), *ring(rows_b, "x"))
    own, other = backward(chunks, row_behind, col_total, pieces, weights)
    own, far = fold_y(spread(fold_core(own, swap(other, "core")), "y"))
    return final(own, swap(far, "zh"), scaled, grad_mixed, features, cotangent)


def solution(mesh):
    split = Mesh(mesh.devices.reshape(2, 2, 4, 4, 4), AXES)
    placed = (P(AXES, None), P(AXES, None), P(), P(), P(AXES, None, None), P(AXES), P(AXES), P(AXES))
    return jax.shard_map(local, mesh=split, in_specs=placed, out_specs=P(AXES, None), check_vma=False)
```

```python
import jax
import jax.numpy as jnp
from jax import lax
from jax.experimental import pallas as pl
from jax.experimental.pallas import tpu as pltpu
from jax.sharding import Mesh
from jax.sharding import PartitionSpec as P

EXPONENT = 2.5
AXES = ("zh", "core", "zl", "x", "y")
TS = 128
H = 256
HALF = 128
CHUNK = 32
STEP = 32
F32 = jnp.float32
BF16 = jnp.bfloat16
VMEM = pltpu.VMEM
MIB = 1 << 20


def shift(value, axis, step):
    return lax.ppermute(value, axis, [(i, (i + step) % 4) for i in range(4)])


def swap(value, axis):
    return lax.ppermute(value, axis, [(0, 1), (1, 0)])


def trade(value, axis, mask):
    return lax.ppermute(value, axis, [(i, i ^ mask) for i in range(4)])


def softplus(value):
    return jnp.maximum(value, 0.0) + jnp.log1p(jnp.exp(-jnp.abs(value)))


def sigmoid(value):
    return 1.0 / (1.0 + jnp.exp(-value))


def vmem_specs(count):
    return [pl.BlockSpec(memory_space=VMEM)] * count


def params(mib):
    return pltpu.CompilerParams(vmem_limit_bytes=mib * MIB)


def shape(dims, dtype=BF16):
    return jax.ShapeDtypeStruct(dims, dtype)


def start_chunks(chunks, most, weights_ref, held, sems):
    for chunk in range(most):
        @pl.when(chunk < chunks)
        def _():
            at = pl.ds(chunk * CHUNK, CHUNK)
            pltpu.make_async_copy(weights_ref.at[at], held.at[at], sems.at[chunk]).start()


def wait_chunk(chunk, weights_ref, held, sems):
    at = pl.ds(chunk * CHUNK, CHUNK)
    pltpu.make_async_copy(weights_ref.at[at], held.at[at], sems.at[chunk]).wait()


def degree_kernel(chunks_ref, row_slot, weights_ref, degree_ref, held, total, sems):
    chunks = chunks_ref[0]
    start_chunks(chunks, held.shape[0] // CHUNK, weights_ref, held, sems)
    total[...] = jnp.zeros_like(total)
    ones = jnp.ones((16, TS), BF16)

    def step(chunk, carry):
        wait_chunk(chunk, weights_ref, held, sems)
        tiles = held[pl.ds(chunk * CHUNK, CHUNK)].reshape(CHUNK * TS, TS)
        sums = lax.dot_general(ones, tiles, (((1,), (1,)), ((), ())), preferred_element_type=F32)
        for lane in range(CHUNK):
            at = pl.ds(row_slot[chunk * CHUNK + lane], 1)
            total[at, :] += sums[:1, lane * TS : lane * TS + TS]
        return carry

    lax.fori_loop(0, chunks, step, 0)
    degree_ref[...] = total[:64]


def degrees(chunks, row_slot, weights):
    slots = weights.shape[0]
    return pl.pallas_call(
        degree_kernel,
        out_shape=shape((64, TS), F32),
        in_specs=[pl.BlockSpec(memory_space=pltpu.SMEM)] * 2 + [pl.BlockSpec(memory_space=pltpu.HBM)],
        out_specs=pl.BlockSpec(memory_space=VMEM),
        scratch_shapes=[
            VMEM(weights.shape, BF16),
            VMEM((72, TS), F32),
            pltpu.SemaphoreType.DMA((slots // CHUNK,)),
        ],
        compiler_params=params(16),
        cost_estimate=pl.CostEstimate(flops=slots * 2 * 16 * TS * TS, bytes_accessed=slots * TS * TS * 2, transcendentals=0),
        name="degrees",
    )(chunks, row_slot, weights)


def strips(body):
    def step(index, carry):
        body(pl.ds(pl.multiple_of(index * 32, 32), 32))
        return carry

    lax.fori_loop(0, TS // 32, step, 0)


def power_kernel(own_ref, far_ref, out_ref):
    def body(rows):
        for index, ref in enumerate((own_ref, far_ref)):
            value = softplus(ref[rows, :].astype(F32))
            out_ref[index, rows, :] = jnp.exp(EXPONENT * jnp.log(value)).astype(BF16)

    strips(body)


def power(own, far):
    return pl.pallas_call(
        power_kernel,
        out_shape=shape((2, *own.shape)),
        in_specs=vmem_specs(2),
        out_specs=pl.BlockSpec(memory_space=VMEM),
        compiler_params=params(8),
        name="power",
    )(own, far)


def stack_kernel(*refs):
    for index, ref in enumerate(refs[:-1]):
        def body(at, carry, index=index, ref=ref):
            refs[-1][index, at] = ref[at]
            return carry

        lax.fori_loop(0, ref.shape[0], body, 0)


def stack(parts):
    return pl.pallas_call(
        stack_kernel,
        out_shape=shape((len(parts), *parts[0].shape)),
        in_specs=vmem_specs(len(parts)),
        out_specs=pl.BlockSpec(memory_space=VMEM),
        compiler_params=params(8),
        name="stack",
    )(*parts)


def halves_kernel(*refs):
    for index, ref in enumerate(refs[:-2]):
        refs[-2][index] = ref[:, :HALF]
        refs[-1][index] = ref[:, HALF:]


def halves(parts):
    return pl.pallas_call(
        halves_kernel,
        out_shape=(shape((len(parts), TS, HALF)), shape((len(parts), TS, HALF))),
        in_specs=vmem_specs(len(parts)),
        out_specs=tuple(vmem_specs(2)),
        compiler_params=params(8),
        name="halves",
    )(*parts)


def forward_kernel(chunks_ref, row_slot, col_slot, *rest):
    pieces, degree_ref, weights_ref, rest = rest[:2], rest[2], rest[3], rest[4:]
    out_a, out_b = rest[:5], rest[5:10]
    held, panel, total, sems = rest[10:]
    chunks = chunks_ref[0]
    start_chunks(chunks, held.shape[0] // CHUNK, weights_ref, held, sems)
    for index, piece in enumerate(pieces):
        def copy(at, carry, index=index, piece=piece):
            for part in range(2):
                panel[index * 8 + at * 2 + part] = piece[at, part]
            return carry

        lax.fori_loop(0, 4, copy, 0)

    def clear(at, carry):
        total[at] = jnp.zeros((TS, H), F32)
        return carry

    lax.fori_loop(0, 64, clear, 0, unroll=4)

    def step(chunk, carry):
        wait_chunk(chunk, weights_ref, held, sems)
        def some(part, carry):
            for lane in range(STEP):
                slot = chunk * CHUNK + part * STEP + lane
                at = row_slot[slot]
                total[at] += jnp.dot(held[slot], panel[col_slot[slot]], preferred_element_type=F32)
            return carry

        return lax.fori_loop(0, CHUNK // STEP, some, carry)

    lax.fori_loop(0, chunks, step, 0)
    def target(outs, slab, part):
        if slab < 2:
            return outs[slab], part * 512
        if slab == 2:
            return outs[2 + part // 2], part % 2 * 512
        return outs[4], part * 512

    for dy in range(4):
        for dx in range(4):
            ref_a, base_a = target(out_a, dy, dx)
            ref_b, base_b = target(out_b, dx, dy)

            def put(dz, carry):
                value = total[dy * 16 + dx * 4 + dz].astype(BF16)
                ref_a[pl.ds(base_a + dz * TS, TS), :] = value[:, :HALF]
                ref_b[pl.ds(base_b + dz * TS, TS), :] = value[:, HALF:]
                return carry

            lax.fori_loop(0, 4, put, 0, unroll=2)
        degree = degree_ref[dy * 16 : dy * 16 + 16]
        high = degree.astype(BF16)
        ref = out_a[(0, 1, 2, 4)[dy]]
        base = ref.shape[0] - 32
        ref[base : base + 16, :] = high
        ref[base + 16 : base + 32, :] = (degree - high.astype(F32)).astype(BF16)


def forward(chunks, row_slot, col_slot, parts, degree, weights):
    slots = weights.shape[0]
    return pl.pallas_call(
        forward_kernel,
        out_shape=tuple(shape((rows, HALF)) for rows in (2080, 2080, 1056, 1024, 2080, 2048, 2048, 1024, 1024, 2048)),
        in_specs=[pl.BlockSpec(memory_space=pltpu.SMEM)] * 3 + vmem_specs(3) + [pl.BlockSpec(memory_space=pltpu.HBM)],
        out_specs=tuple(vmem_specs(10)),
        scratch_shapes=[
            VMEM(weights.shape, BF16),
            VMEM((16, TS, H), BF16),
            VMEM((65, TS, H), F32),
            pltpu.SemaphoreType.DMA((slots // CHUNK,)),
        ],
        compiler_params=params(40),
        cost_estimate=pl.CostEstimate(flops=slots * 2 * TS * TS * H, bytes_accessed=slots * TS * TS * 2, transcendentals=0),
        name="forward",
    )(chunks, row_slot, col_slot, *parts, degree, weights)


def blocks(count, body):
    def step(index, carry):
        body(pl.ds(pl.multiple_of(index * TS, TS), TS))
        return carry

    lax.fori_loop(0, count, step, 0)


def sum_refs(refs, at):
    total = refs[0][at].astype(F32)
    for ref in refs[1:]:
        total = total + ref[at].astype(F32)
    return total


def split_degree(degree, rows):
    high = degree.astype(BF16).astype(F32)
    pieces = [high, degree - high]
    have = 2 * degree.shape[0]
    if have < rows:
        pieces.append(jnp.zeros((rows - have, degree.shape[1]), F32))
    return jnp.concatenate(pieces, axis=0).astype(BF16)


def fold_kernel(with_degree, *refs):
    parts, outs = refs[:-4], refs[-4:]
    for index, out in enumerate(outs):
        def body(rows, out=out, index=index):
            out[rows, :] = sum_refs(parts, (pl.ds(rows.start + index * 512, TS), slice(None))).astype(BF16)

        blocks(4, body)
    if with_degree:
        tail = sum_refs(parts, (slice(2048, 2080), slice(None)))
        degree = tail[:16] + tail[16:]
        for index, out in enumerate(outs):
            out[512:528, :] = split_degree(degree[index * 4 : index * 4 + 4], 16)


def fold(parts, with_degree):
    rows = 528 if with_degree else 512
    return pl.pallas_call(
        lambda *refs: fold_kernel(with_degree, *refs),
        out_shape=tuple([shape((rows, HALF))] * 4),
        in_specs=vmem_specs(len(parts)),
        out_specs=tuple(vmem_specs(4)),
        compiler_params=params(8),
        name="fold",
    )(*parts)


def relay_kernel(with_degree, behind_ref, ahead_ref, got_first, got_last, out_behind, out_ahead):
    def body(rows):
        later = pl.ds(rows.start + 1024, TS)
        out_behind[rows, :] = sum_refs((behind_ref, got_first), (rows, slice(None))).astype(BF16)
        out_behind[later, :] = behind_ref[later, :]
        out_ahead[rows, :] = ahead_ref[rows, :]
        out_ahead[later, :] = (ahead_ref[later, :].astype(F32) + got_last[rows, :].astype(F32)).astype(BF16)

    blocks(8, body)
    if with_degree:
        tail = behind_ref[2048:2080, :].astype(F32) + got_first[1024:1056, :].astype(F32)
        out_behind[2048:2080, :] = split_degree(tail[:16] + tail[16:], 32)
        out_ahead[2048:2080, :] = ahead_ref[2048:2080, :]


def relay(behind, ahead, got_first, got_last, with_degree):
    return pl.pallas_call(
        lambda *refs: relay_kernel(with_degree, *refs),
        out_shape=(shape(behind.shape), shape(ahead.shape)),
        in_specs=vmem_specs(4),
        out_specs=tuple(vmem_specs(2)),
        compiler_params=params(8),
        name="relay",
    )(behind, ahead, got_first, got_last)


def add_kernel(p0, p1, out_ref):
    def body(rows):
        out_ref[rows, :] = sum_refs((p0, p1), (rows, slice(None)))

    blocks(4, body)


def add(parts):
    return pl.pallas_call(
        add_kernel,
        out_shape=shape(parts[0].shape, F32),
        in_specs=vmem_specs(2),
        out_specs=pl.BlockSpec(memory_space=VMEM),
        compiler_params=params(8),
        name="add",
    )(*parts)


def pair_kernel(odd_ref, *refs):
    parts, keep, send = refs[:3], refs[3], refs[4]
    odd = odd_ref[0]
    for out, base, place in ((keep, 0, 0), (keep, 512, 3 - 2 * odd), (send, 0, 1 + 2 * odd), (send, 512, 2)):
        def body(rows, out=out, base=base, place=place):
            at = pl.ds(pl.multiple_of(place * 512 + rows.start, TS), TS)
            out[pl.ds(rows.start + base, TS), :] = sum_refs(parts, (at, slice(None))).astype(BF16)

        blocks(4, body)


def pair(odd, parts):
    return pl.pallas_call(
        pair_kernel,
        out_shape=(shape((1024, HALF)), shape((1024, HALF))),
        in_specs=[pl.BlockSpec(memory_space=pltpu.SMEM)] + vmem_specs(3),
        out_specs=tuple(vmem_specs(2)),
        compiler_params=params(8),
        name="pair",
    )(odd, *parts)


def middle_kernel(keep_ref, got_ref, own_ref, send_ref):
    half = keep_ref.shape[0] // 2

    def body(rows):
        later = pl.ds(rows.start + half, TS)
        own_ref[rows, :] = keep_ref[rows, :].astype(F32) + got_ref[rows, :].astype(F32)
        send_ref[rows, :] = (keep_ref[later, :].astype(F32) + got_ref[later, :].astype(F32)).astype(BF16)

    blocks(half // TS, body)


def pairwise(keep, send, axis):
    half, width = keep.shape[0] // 2, keep.shape[1]
    own, send = pl.pallas_call(
        middle_kernel,
        out_shape=(shape((half, width), F32), shape((half, width))),
        in_specs=vmem_specs(2),
        out_specs=tuple(vmem_specs(2)),
        compiler_params=params(8),
        name="middle",
    )(keep, trade(send, axis, 1))
    return own, trade(send, axis, 3)


def join_kernel(*refs):
    parts_a, sums_b, outs = refs[:4], refs[4], refs[5:]
    tail = sum_refs(parts_a, (slice(512, 528), slice(None)))
    degree = tail[0:4] + tail[4:8]
    high = degree.astype(BF16).astype(F32)
    low = degree - high
    for index, out in enumerate(outs):
        rows = (slice(index * TS, index * TS + TS), slice(None))
        out[0:TS, :HALF] = sum_refs(parts_a, rows).astype(BF16)
        out[0:TS, HALF:] = sums_b[rows].astype(BF16)
        out[TS : TS + 16, :HALF] = jnp.broadcast_to(high[index : index + 1], (16, HALF)).astype(BF16)
        out[TS : TS + 16, HALF:] = jnp.broadcast_to(low[index : index + 1], (16, HALF)).astype(BF16)


def join(parts_a, sums_b):
    return pl.pallas_call(
        join_kernel,
        out_shape=tuple([shape((TS + 16, H))] * 4),
        in_specs=vmem_specs(5),
        out_specs=tuple(vmem_specs(4)),
        compiler_params=params(8),
        name="join",
    )(*parts_a, sums_b)


def terms_kernel(p0, p1, p2, p3, features_ref, cotangent_ref, first_ref, second_ref, scaled_ref, grad_ref, half_ref):
    parts = (p0, p1, p2, p3)
    neighbour = sum_refs(parts, (slice(0, TS), slice(None)))
    tail = sum_refs(parts, (slice(TS, TS + 16), slice(None)))
    degree = tail[0:1, :HALF] + tail[0:1, HALF:]
    column = 1.0 + jnp.broadcast_to(degree, (TS, HALF)).T
    denominator = jnp.concatenate([column, column], axis=1)
    as_float = features_ref[...].astype(F32)
    powered = jnp.exp(EXPONENT * jnp.log(softplus(as_float)))
    mean_pow = (powered + neighbour) / denominator
    aggregated = jnp.exp(jnp.log(mean_pow) / EXPONENT)
    mixed = (aggregated + as_float).astype(BF16)
    pre_act = jnp.dot(mixed, first_ref[...], preferred_element_type=F32)
    grad_act = lax.dot_general(cotangent_ref[...], second_ref[...], (((1,), (1,)), ((), ())), preferred_element_type=F32)
    gate = sigmoid(pre_act)
    grad_pre = (grad_act * gate * (1.0 + pre_act * (1.0 - gate))).astype(BF16)
    grad_mixed = lax.dot_general(grad_pre, first_ref[...], (((1,), (1,)), ((), ())), preferred_element_type=F32)
    scaled = grad_mixed * aggregated / (EXPONENT * mean_pow) / denominator
    scaled_ref[...] = scaled
    grad_ref[...] = grad_mixed
    half_ref[...] = scaled.astype(BF16)


def terms(parts, features, cotangent, first, second):
    return pl.pallas_call(
        terms_kernel,
        out_shape=(shape((TS, H), F32), shape((TS, H), F32), shape((TS, H))),
        in_specs=vmem_specs(8),
        out_specs=tuple(vmem_specs(3)),
        compiler_params=params(16),
        name="terms",
    )(*parts, features, cotangent, first, second)


def place_kernel(*refs):
    pieces, source, sems = refs[:6], refs[6], refs[7]
    low, high = pl.ds(0, HALF), pl.ds(HALF, HALF)
    targets = [source.at[slab, :, :, :, low] for slab in (0, 1, 3)]
    targets += [source.at[:, slab, :, :, high] for slab in (0, 1, 3)]
    copies = [pltpu.make_async_copy(piece, target, sems.at[i]) for i, (piece, target) in enumerate(zip(pieces, targets))]
    for copy in copies:
        copy.start()
    for copy in copies:
        copy.wait()


def place(pieces):
    return pl.pallas_call(
        place_kernel,
        out_shape=shape((4, 4, 4, TS, H)),
        in_specs=vmem_specs(6),
        out_specs=pl.BlockSpec(memory_space=VMEM),
        scratch_shapes=[pltpu.SemaphoreType.DMA((6,))],
        compiler_params=params(16),
        cost_estimate=pl.CostEstimate(flops=0, bytes_accessed=6 * MIB, transcendentals=0),
        name="place",
    )(*pieces)


def backward_kernel(chunks_ref, row_slot, col_slot, *rest):
    pieces, weights_ref, outs, source = rest[:4], rest[5], rest[6:8], rest[8]
    held, total, sems, piece_sems = rest[9:]
    chunks = chunks_ref[0]
    low, high = pl.ds(0, HALF), pl.ds(HALF, HALF)
    first, last = pl.ds(0, 2), pl.ds(2, 2)
    targets = [source.at[2, part, :, :, low] for part in (first, last)]
    targets += [source.at[part, 2, :, :, high] for part in (first, last)]
    copies = [pltpu.make_async_copy(piece, target, piece_sems.at[i]) for i, (piece, target) in enumerate(zip(pieces, targets))]
    for copy in copies:
        copy.start()
    start_chunks(chunks, held.shape[0] // CHUNK, weights_ref, held, sems)

    def clear(at, carry):
        total[at] = jnp.zeros((TS, H), F32)
        return carry

    lax.fori_loop(0, 16, clear, 0)
    for copy in copies:
        copy.wait()

    def step(chunk, carry):
        wait_chunk(chunk, weights_ref, held, sems)
        def some(part, carry):
            for lane in range(STEP):
                slot = chunk * CHUNK + part * STEP + lane
                at, row = col_slot[slot], row_slot[slot]
                tile = source[row // 16, row // 4 % 4, row % 4]
                total[at] += lax.dot_general(held[slot], tile, (((0,), (0,)), ((), ())), preferred_element_type=F32)
            return carry

        return lax.fori_loop(0, CHUNK // STEP, some, carry)

    lax.fori_loop(0, chunks, step, 0)
    for index, out in enumerate(outs):
        def put(at, carry, out=out, index=index):
            out[at] = total[8 * index + at].astype(BF16)
            return carry

        lax.fori_loop(0, 8, put, 0)


def backward(chunks, row_slot, col_slot, pieces, source, weights):
    slots = weights.shape[0]
    return pl.pallas_call(
        backward_kernel,
        out_shape=(shape((8, TS, H)), shape((8, TS, H)), shape(source.shape)),
        in_specs=[pl.BlockSpec(memory_space=pltpu.SMEM)] * 3 + vmem_specs(5) + [pl.BlockSpec(memory_space=pltpu.HBM)],
        out_specs=tuple(vmem_specs(3)),
        scratch_shapes=[
            VMEM(weights.shape, BF16),
            VMEM((17, TS, H), F32),
            pltpu.SemaphoreType.DMA((slots // CHUNK,)),
            pltpu.SemaphoreType.DMA((4,)),
        ],
        input_output_aliases={7: 2},
        compiler_params=params(32),
        cost_estimate=pl.CostEstimate(flops=slots * 2 * TS * TS * H, bytes_accessed=slots * TS * TS * 2, transcendentals=0),
        name="backward",
    )(chunks, row_slot, col_slot, *pieces, source, weights)[:2]


def fold_core_kernel(own_ref, got_ref, *outs):
    for index, out in enumerate(outs):
        at = index % 4 * 2 + index // 4
        out[...] = (own_ref[at].astype(F32) + got_ref[at].astype(F32)).astype(BF16)


def fold_core(own, got):
    return pl.pallas_call(
        fold_core_kernel,
        out_shape=tuple([shape((TS, H))] * 8),
        in_specs=vmem_specs(2),
        out_specs=tuple(vmem_specs(8)),
        compiler_params=params(8),
        name="fold_core",
    )(own, got)


def fold_y_kernel(p0, p1, p2, p3, out_ref):
    out_ref[...] = sum_refs((p0, p1, p2, p3), slice(None)).astype(BF16)


def fold_y(parts):
    return pl.pallas_call(
        fold_y_kernel,
        out_shape=shape((TS, H)),
        in_specs=vmem_specs(4),
        out_specs=pl.BlockSpec(memory_space=VMEM),
        compiler_params=params(8),
        name="fold_y",
    )(*parts)


def final_kernel(p0, p1, p2, p3, got_ref, scaled_ref, grad_ref, features_ref, cotangent_ref, out_ref):
    def body(rows):
        as_float = features_ref[rows, :].astype(F32)
        messages = softplus(as_float)
        powered = jnp.exp(EXPONENT * jnp.log(messages))
        back_sums = sum_refs((p0, p1, p2, p3, got_ref), (rows, slice(None)))
        grad_message = (scaled_ref[rows, :] + back_sums) * (EXPONENT * powered / messages) * sigmoid(as_float)
        out_ref[rows, :] = cotangent_ref[rows, :].astype(F32) + grad_ref[rows, :] + grad_message

    strips(body)


def final(parts, got, scaled, grad, features, cotangent):
    return pl.pallas_call(
        final_kernel,
        out_shape=shape((TS, H), F32),
        in_specs=vmem_specs(9),
        out_specs=pl.BlockSpec(memory_space=VMEM),
        compiler_params=params(8),
        name="final",
    )(*parts, got, scaled, grad, features, cotangent)


def direct(value, axis):
    return [value] + [shift(value, axis, step) for step in (1, 2, 3)]


def ring(value, axis):
    behind, ahead = shift(value, axis, 1), shift(value, axis, 3)
    return value, behind, shift(behind[:2], axis, 1), shift(ahead[2:], axis, 3), ahead


def ring_sums(slabs, axis, with_degree):
    own, behind, first, last, ahead = slabs
    got_first, got_last = shift(first, axis, 1), shift(last, axis, 3)
    behind, ahead = relay(behind, ahead, got_first, got_last, with_degree)
    return own, shift(behind, axis, 1), shift(ahead, axis, 3)


def spread(slabs, axis):
    return [slabs[0]] + [shift(slabs[step], axis, step) for step in (1, 2, 3)]


def local(features, cotangent, w_first, w_second, weights, tile_rows, tile_cols, tile_counts):
    slots = weights.shape[0]
    zh, core, zl, x, y = (lax.axis_index(axis) for axis in AXES)
    live = jnp.arange(slots, dtype=jnp.int32) < tile_counts[0]
    chunks = (tile_counts + CHUNK - 1) // CHUNK
    row_z, row_x, row_y = tile_rows // 16, tile_rows // 4 % 4, tile_rows % 4
    row_ahead = ((row_y - y) & 3) * 16 + ((row_x - x) & 3) * 4 + ((row_z - zl) & 3)
    row_behind = ((y - row_y) & 3) * 16 + ((x - row_x) & 3) * 4 + ((zl - row_z) & 3)
    col_h, col_core, col_y = tile_cols // 8, tile_cols // 4 % 2, tile_cols % 4
    col_base = (col_core ^ core) * 8 + (col_h ^ zh)
    row_total = jnp.where(live, row_ahead, 64)
    col_panel = col_base + ((y - col_y) & 3) * 2
    col_total = jnp.where(live, (col_core ^ core) * 8 + ((col_y - y) & 3) * 2 + (col_h ^ zh), 16)
    weights = pltpu.with_memory_space_constraint(weights, pltpu.HBM)

    far = swap(features, "zh")
    degree = degrees(chunks, row_total, weights)
    far, degree, col_panel = lax.optimization_barrier((far, degree, col_panel))
    panels = stack(direct(power(features, far), "y"))
    slabs = forward(chunks, row_total, col_panel, (panels, swap(panels, "core")), degree, weights)
    odd = (y & 1).astype(jnp.int32).reshape(1)
    slabs_a = fold(ring_sums(slabs[:5], "y", True), True)
    sums_b = add(pairwise(*pair(odd, ring_sums(slabs[5:], "x", False)), "y"))
    slabs = join(spread(slabs_a, "x"), sums_b)
    scaled, grad_mixed, scaled_half = terms(spread(slabs, "zl"), features, cotangent, w_first, w_second)

    rows_a, rows_b = halves(direct(scaled_half, "zl"))
    rows_a = stack(direct(rows_a, "x"))
    rows_b = stack(direct(rows_b, "y"))
    pieces = (*ring(rows_a, "y"), *ring(rows_b, "x"))
    source = place([pieces[at] for at in (0, 1, 4, 5, 6, 9)])
    pieces = [pieces[at] for at in (2, 3, 7, 8)]
    own, other = backward(chunks, row_behind, col_total, pieces, source, weights)
    slabs = fold_core(own, swap(other, "core"))
    far = fold_y(spread(slabs[4:], "y"))
    return final(spread(slabs[:4], "y"), swap(far, "zh"), scaled, grad_mixed, features, cotangent)


def solution(mesh):
    split = Mesh(mesh.devices.reshape(2, 2, 4, 4, 4), AXES)
    placed = (P(AXES, None), P(AXES, None), P(), P(), P(AXES, None, None), P(AXES), P(AXES), P(AXES))
    return jax.shard_map(local, mesh=split, in_specs=placed, out_specs=P(AXES, None), check_vma=False)
```

```python
import jax
import jax.numpy as jnp
from jax import lax
from jax.experimental import pallas as pl
from jax.experimental.pallas import tpu as pltpu
from jax.sharding import Mesh
from jax.sharding import PartitionSpec as P

EXPONENT = 2.5
AXES = ("zh", "core", "zl", "x", "y")
TS = 128
H = 256
HALF = 128
CHUNK = 32
STEP = 32
F32 = jnp.float32
BF16 = jnp.bfloat16
VMEM = pltpu.VMEM
MIB = 1 << 20


def shift(value, axis, step):
    return lax.ppermute(value, axis, [(i, (i + step) % 4) for i in range(4)])


def swap(value, axis):
    return lax.ppermute(value, axis, [(0, 1), (1, 0)])


def trade(value, axis, mask):
    return lax.ppermute(value, axis, [(i, i ^ mask) for i in range(4)])


def softplus(value):
    return jnp.maximum(value, 0.0) + jnp.log1p(jnp.exp(-jnp.abs(value)))


def sigmoid(value):
    return 1.0 / (1.0 + jnp.exp(-value))


def vmem_specs(count):
    return [pl.BlockSpec(memory_space=VMEM)] * count


def params(mib):
    return pltpu.CompilerParams(vmem_limit_bytes=mib * MIB)


def shape(dims, dtype=BF16):
    return jax.ShapeDtypeStruct(dims, dtype)


def start_chunks(chunks, most, weights_ref, held, sems):
    for chunk in range(most):
        @pl.when(chunk < chunks)
        def _():
            at = pl.ds(chunk * CHUNK, CHUNK)
            pltpu.make_async_copy(weights_ref.at[at], held.at[at], sems.at[chunk]).start()


def wait_chunk(chunk, weights_ref, held, sems):
    at = pl.ds(chunk * CHUNK, CHUNK)
    pltpu.make_async_copy(weights_ref.at[at], held.at[at], sems.at[chunk]).wait()


def degree_kernel(chunks_ref, row_slot, weights_ref, degree_ref, held, total, sems):
    chunks = chunks_ref[0]
    start_chunks(chunks, held.shape[0] // CHUNK, weights_ref, held, sems)
    total[...] = jnp.zeros_like(total)
    ones = jnp.ones((16, TS), BF16)

    def step(chunk, carry):
        wait_chunk(chunk, weights_ref, held, sems)
        tiles = held[pl.ds(chunk * CHUNK, CHUNK)].reshape(CHUNK * TS, TS)
        sums = lax.dot_general(ones, tiles, (((1,), (1,)), ((), ())), preferred_element_type=F32)
        for lane in range(CHUNK):
            at = pl.ds(row_slot[chunk * CHUNK + lane], 1)
            total[at, :] += sums[:1, lane * TS : lane * TS + TS]
        return carry

    lax.fori_loop(0, chunks, step, 0)
    degree_ref[...] = total[:64]


def degrees(chunks, row_slot, weights):
    slots = weights.shape[0]
    return pl.pallas_call(
        degree_kernel,
        out_shape=shape((64, TS), F32),
        in_specs=[pl.BlockSpec(memory_space=pltpu.SMEM)] * 2 + [pl.BlockSpec(memory_space=pltpu.HBM)],
        out_specs=pl.BlockSpec(memory_space=VMEM),
        scratch_shapes=[
            VMEM(weights.shape, BF16),
            VMEM((72, TS), F32),
            pltpu.SemaphoreType.DMA((slots // CHUNK,)),
        ],
        compiler_params=params(16),
        cost_estimate=pl.CostEstimate(flops=slots * 2 * 16 * TS * TS, bytes_accessed=slots * TS * TS * 2, transcendentals=0),
        name="degrees",
    )(chunks, row_slot, weights)


def strips(body):
    def step(index, carry):
        body(pl.ds(pl.multiple_of(index * 32, 32), 32))
        return carry

    lax.fori_loop(0, TS // 32, step, 0)


def power_kernel(own_ref, far_ref, out_ref):
    def body(rows):
        for index, ref in enumerate((own_ref, far_ref)):
            value = softplus(ref[rows, :].astype(F32))
            out_ref[index, rows, :] = jnp.exp(EXPONENT * jnp.log(value)).astype(BF16)

    strips(body)


def power(own, far):
    return pl.pallas_call(
        power_kernel,
        out_shape=shape((2, *own.shape)),
        in_specs=vmem_specs(2),
        out_specs=pl.BlockSpec(memory_space=VMEM),
        compiler_params=params(8),
        name="power",
    )(own, far)


def stack_kernel(*refs):
    for index, ref in enumerate(refs[:-1]):
        def body(at, carry, index=index, ref=ref):
            refs[-1][index, at] = ref[at]
            return carry

        lax.fori_loop(0, ref.shape[0], body, 0)


def stack(parts):
    return pl.pallas_call(
        stack_kernel,
        out_shape=shape((len(parts), *parts[0].shape)),
        in_specs=vmem_specs(len(parts)),
        out_specs=pl.BlockSpec(memory_space=VMEM),
        compiler_params=params(8),
        name="stack",
    )(*parts)


def halves_kernel(*refs):
    for index, ref in enumerate(refs[:-2]):
        refs[-2][index] = ref[:, :HALF]
        refs[-1][index] = ref[:, HALF:]


def halves(parts):
    return pl.pallas_call(
        halves_kernel,
        out_shape=(shape((len(parts), TS, HALF)), shape((len(parts), TS, HALF))),
        in_specs=vmem_specs(len(parts)),
        out_specs=tuple(vmem_specs(2)),
        compiler_params=params(8),
        name="halves",
    )(*parts)


def forward_kernel(chunks_ref, row_slot, col_slot, *rest):
    pieces, degree_ref, weights_ref, rest = rest[:2], rest[2], rest[3], rest[4:]
    out_a, out_b = rest[:5], rest[5:10]
    held, panel, total, sems = rest[10:]
    chunks = chunks_ref[0]
    start_chunks(chunks, held.shape[0] // CHUNK, weights_ref, held, sems)
    for index, piece in enumerate(pieces):
        def copy(at, carry, index=index, piece=piece):
            for part in range(2):
                panel[index * 8 + at * 2 + part] = piece[at, part]
            return carry

        lax.fori_loop(0, 4, copy, 0)

    def clear(at, carry):
        total[at] = jnp.zeros((TS, H), F32)
        return carry

    lax.fori_loop(0, 64, clear, 0, unroll=4)

    def step(chunk, carry):
        wait_chunk(chunk, weights_ref, held, sems)
        def some(part, carry):
            for lane in range(STEP):
                slot = chunk * CHUNK + part * STEP + lane
                at = row_slot[slot]
                total[at] += jnp.dot(held[slot], panel[col_slot[slot]], preferred_element_type=F32)
            return carry

        return lax.fori_loop(0, CHUNK // STEP, some, carry)

    lax.fori_loop(0, chunks, step, 0)
    def target(outs, slab, part):
        if slab < 2:
            return outs[slab], part * 512
        if slab == 2:
            return outs[2 + part // 2], part % 2 * 512
        return outs[4], part * 512

    for dy in range(4):
        for dx in range(4):
            ref_a, base_a = target(out_a, dy, dx)
            ref_b, base_b = target(out_b, dx, dy)

            def put(dz, carry):
                value = total[dy * 16 + dx * 4 + dz].astype(BF16)
                ref_a[pl.ds(base_a + dz * TS, TS), :] = value[:, :HALF]
                ref_b[pl.ds(base_b + dz * TS, TS), :] = value[:, HALF:]
                return carry

            lax.fori_loop(0, 4, put, 0, unroll=2)
        degree = degree_ref[dy * 16 : dy * 16 + 16]
        high = degree.astype(BF16)
        ref = out_a[(0, 1, 2, 4)[dy]]
        base = ref.shape[0] - 32
        ref[base : base + 16, :] = high
        ref[base + 16 : base + 32, :] = (degree - high.astype(F32)).astype(BF16)


def forward(chunks, row_slot, col_slot, parts, degree, weights):
    slots = weights.shape[0]
    return pl.pallas_call(
        forward_kernel,
        out_shape=tuple(shape((rows, HALF)) for rows in (2080, 2080, 1056, 1024, 2080, 2048, 2048, 1024, 1024, 2048)),
        in_specs=[pl.BlockSpec(memory_space=pltpu.SMEM)] * 3 + vmem_specs(3) + [pl.BlockSpec(memory_space=pltpu.HBM)],
        out_specs=tuple(vmem_specs(10)),
        scratch_shapes=[
            VMEM(weights.shape, BF16),
            VMEM((16, TS, H), BF16),
            VMEM((65, TS, H), F32),
            pltpu.SemaphoreType.DMA((slots // CHUNK,)),
        ],
        compiler_params=params(28),
        cost_estimate=pl.CostEstimate(flops=slots * 2 * TS * TS * H, bytes_accessed=slots * TS * TS * 2, transcendentals=0),
        name="forward",
    )(chunks, row_slot, col_slot, *parts, degree, weights)


def blocks(count, body):
    def step(index, carry):
        body(pl.ds(pl.multiple_of(index * TS, TS), TS))
        return carry

    lax.fori_loop(0, count, step, 0)


def sum_refs(refs, at):
    total = refs[0][at].astype(F32)
    for ref in refs[1:]:
        total = total + ref[at].astype(F32)
    return total


def split_degree(degree, rows):
    high = degree.astype(BF16).astype(F32)
    pieces = [high, degree - high]
    have = 2 * degree.shape[0]
    if have < rows:
        pieces.append(jnp.zeros((rows - have, degree.shape[1]), F32))
    return jnp.concatenate(pieces, axis=0).astype(BF16)


def fold_kernel(with_degree, *refs):
    parts, outs = refs[:-4], refs[-4:]
    for index, out in enumerate(outs):
        def body(rows, out=out, index=index):
            out[rows, :] = sum_refs(parts, (pl.ds(rows.start + index * 512, TS), slice(None))).astype(BF16)

        blocks(4, body)
    if with_degree:
        tail = sum_refs(parts, (slice(2048, 2080), slice(None)))
        degree = tail[:16] + tail[16:]
        for index, out in enumerate(outs):
            out[512:528, :] = split_degree(degree[index * 4 : index * 4 + 4], 16)


def fold(parts, with_degree):
    rows = 528 if with_degree else 512
    return pl.pallas_call(
        lambda *refs: fold_kernel(with_degree, *refs),
        out_shape=tuple([shape((rows, HALF))] * 4),
        in_specs=vmem_specs(len(parts)),
        out_specs=tuple(vmem_specs(4)),
        compiler_params=params(8),
        name="fold",
    )(*parts)


def relay_kernel(with_degree, behind_ref, ahead_ref, got_first, got_last, out_behind, out_ahead):
    def body(rows):
        later = pl.ds(rows.start + 1024, TS)
        out_behind[rows, :] = sum_refs((behind_ref, got_first), (rows, slice(None))).astype(BF16)
        out_behind[later, :] = behind_ref[later, :]
        out_ahead[rows, :] = ahead_ref[rows, :]
        out_ahead[later, :] = (ahead_ref[later, :].astype(F32) + got_last[rows, :].astype(F32)).astype(BF16)

    blocks(8, body)
    if with_degree:
        tail = behind_ref[2048:2080, :].astype(F32) + got_first[1024:1056, :].astype(F32)
        out_behind[2048:2080, :] = split_degree(tail[:16] + tail[16:], 32)
        out_ahead[2048:2080, :] = ahead_ref[2048:2080, :]


def relay(behind, ahead, got_first, got_last, with_degree):
    return pl.pallas_call(
        lambda *refs: relay_kernel(with_degree, *refs),
        out_shape=(VMEM(behind.shape, BF16), VMEM(ahead.shape, BF16)),
        in_specs=vmem_specs(4),
        out_specs=tuple(vmem_specs(2)),
        compiler_params=params(8),
        name="relay",
    )(behind, ahead, got_first, got_last)


def add_kernel(p0, p1, out_ref):
    def body(rows):
        out_ref[rows, :] = sum_refs((p0, p1), (rows, slice(None)))

    blocks(4, body)


def add(parts):
    return pl.pallas_call(
        add_kernel,
        out_shape=shape(parts[0].shape, F32),
        in_specs=vmem_specs(2),
        out_specs=pl.BlockSpec(memory_space=VMEM),
        compiler_params=params(8),
        name="add",
    )(*parts)


def pair_kernel(odd_ref, *refs):
    parts, keep, send = refs[:3], refs[3], refs[4]
    odd = odd_ref[0]
    for out, base, place in ((keep, 0, 0), (keep, 512, 3 - 2 * odd), (send, 0, 1 + 2 * odd), (send, 512, 2)):
        def body(rows, out=out, base=base, place=place):
            at = pl.ds(pl.multiple_of(place * 512 + rows.start, TS), TS)
            out[pl.ds(rows.start + base, TS), :] = sum_refs(parts, (at, slice(None))).astype(BF16)

        blocks(4, body)


def pair(odd, parts):
    return pl.pallas_call(
        pair_kernel,
        out_shape=(shape((1024, HALF)), shape((1024, HALF))),
        in_specs=[pl.BlockSpec(memory_space=pltpu.SMEM)] + vmem_specs(3),
        out_specs=tuple(vmem_specs(2)),
        compiler_params=params(8),
        name="pair",
    )(odd, *parts)


def middle_kernel(keep_ref, got_ref, own_ref, send_ref):
    half = keep_ref.shape[0] // 2

    def body(rows):
        later = pl.ds(rows.start + half, TS)
        own_ref[rows, :] = keep_ref[rows, :].astype(F32) + got_ref[rows, :].astype(F32)
        send_ref[rows, :] = (keep_ref[later, :].astype(F32) + got_ref[later, :].astype(F32)).astype(BF16)

    blocks(half // TS, body)


def pairwise(keep, send, axis):
    half, width = keep.shape[0] // 2, keep.shape[1]
    own, send = pl.pallas_call(
        middle_kernel,
        out_shape=(shape((half, width), F32), shape((half, width))),
        in_specs=vmem_specs(2),
        out_specs=tuple(vmem_specs(2)),
        compiler_params=params(8),
        name="middle",
    )(keep, trade(send, axis, 1))
    return own, trade(send, axis, 3)


def join_kernel(*refs):
    parts_a, sums_b, outs = refs[:4], refs[4], refs[5:]
    tail = sum_refs(parts_a, (slice(512, 528), slice(None)))
    degree = tail[0:4] + tail[4:8]
    high = degree.astype(BF16).astype(F32)
    low = degree - high
    for index, out in enumerate(outs):
        rows = (slice(index * TS, index * TS + TS), slice(None))
        out[0:TS, :HALF] = sum_refs(parts_a, rows).astype(BF16)
        out[0:TS, HALF:] = sums_b[rows].astype(BF16)
        out[TS : TS + 16, :HALF] = jnp.broadcast_to(high[index : index + 1], (16, HALF)).astype(BF16)
        out[TS : TS + 16, HALF:] = jnp.broadcast_to(low[index : index + 1], (16, HALF)).astype(BF16)


def join(parts_a, sums_b):
    return pl.pallas_call(
        join_kernel,
        out_shape=tuple([shape((TS + 16, H))] * 4),
        in_specs=vmem_specs(5),
        out_specs=tuple(vmem_specs(4)),
        compiler_params=params(8),
        name="join",
    )(*parts_a, sums_b)


def terms_kernel(p0, p1, p2, p3, features_ref, cotangent_ref, first_ref, second_ref, scaled_ref, grad_ref, half_ref):
    parts = (p0, p1, p2, p3)
    neighbour = sum_refs(parts, (slice(0, TS), slice(None)))
    tail = sum_refs(parts, (slice(TS, TS + 16), slice(None)))
    degree = tail[0:1, :HALF] + tail[0:1, HALF:]
    column = 1.0 + jnp.broadcast_to(degree, (TS, HALF)).T
    denominator = jnp.concatenate([column, column], axis=1)
    as_float = features_ref[...].astype(F32)
    powered = jnp.exp(EXPONENT * jnp.log(softplus(as_float)))
    mean_pow = (powered + neighbour) / denominator
    aggregated = jnp.exp(jnp.log(mean_pow) / EXPONENT)
    mixed = (aggregated + as_float).astype(BF16)
    pre_act = jnp.dot(mixed, first_ref[...], preferred_element_type=F32)
    grad_act = lax.dot_general(cotangent_ref[...], second_ref[...], (((1,), (1,)), ((), ())), preferred_element_type=F32)
    gate = sigmoid(pre_act)
    grad_pre = (grad_act * gate * (1.0 + pre_act * (1.0 - gate))).astype(BF16)
    grad_mixed = lax.dot_general(grad_pre, first_ref[...], (((1,), (1,)), ((), ())), preferred_element_type=F32)
    scaled = grad_mixed * aggregated / (EXPONENT * mean_pow) / denominator
    scaled_ref[...] = scaled
    grad_ref[...] = grad_mixed
    half_ref[...] = scaled.astype(BF16)


def terms(parts, features, cotangent, first, second):
    return pl.pallas_call(
        terms_kernel,
        out_shape=(shape((TS, H), F32), shape((TS, H), F32), shape((TS, H))),
        in_specs=vmem_specs(8),
        out_specs=tuple(vmem_specs(3)),
        compiler_params=params(16),
        name="terms",
    )(*parts, features, cotangent, first, second)


def place_kernel(*refs):
    pieces, source, sems = refs[:6], refs[6], refs[7]
    low, high = pl.ds(0, HALF), pl.ds(HALF, HALF)
    targets = [source.at[slab, :, :, :, low] for slab in (0, 1, 3)]
    targets += [source.at[:, slab, :, :, high] for slab in (0, 1, 3)]
    copies = [pltpu.make_async_copy(piece, target, sems.at[i]) for i, (piece, target) in enumerate(zip(pieces, targets))]
    for copy in copies:
        copy.start()
    for copy in copies:
        copy.wait()


def place(pieces):
    return pl.pallas_call(
        place_kernel,
        out_shape=shape((4, 4, 4, TS, H)),
        in_specs=vmem_specs(6),
        out_specs=pl.BlockSpec(memory_space=VMEM),
        scratch_shapes=[pltpu.SemaphoreType.DMA((6,))],
        compiler_params=params(16),
        cost_estimate=pl.CostEstimate(flops=0, bytes_accessed=6 * MIB, transcendentals=0),
        name="place",
    )(*pieces)


def backward_kernel(chunks_ref, row_slot, col_slot, *rest):
    pieces, weights_ref, outs, source = rest[:4], rest[5], rest[6:8], rest[8]
    held, total, sems, piece_sems = rest[9:]
    chunks = chunks_ref[0]
    low, high = pl.ds(0, HALF), pl.ds(HALF, HALF)
    first, last = pl.ds(0, 2), pl.ds(2, 2)
    targets = [source.at[2, part, :, :, low] for part in (first, last)]
    targets += [source.at[part, 2, :, :, high] for part in (first, last)]
    copies = [pltpu.make_async_copy(piece, target, piece_sems.at[i]) for i, (piece, target) in enumerate(zip(pieces, targets))]
    for copy in copies:
        copy.start()
    start_chunks(chunks, held.shape[0] // CHUNK, weights_ref, held, sems)

    def clear(at, carry):
        total[at] = jnp.zeros((TS, H), F32)
        return carry

    lax.fori_loop(0, 16, clear, 0)
    for copy in copies:
        copy.wait()

    def step(chunk, carry):
        wait_chunk(chunk, weights_ref, held, sems)
        def some(part, carry):
            for lane in range(STEP):
                slot = chunk * CHUNK + part * STEP + lane
                at, row = col_slot[slot], row_slot[slot]
                tile = source[row // 16, row // 4 % 4, row % 4]
                total[at] += lax.dot_general(held[slot], tile, (((0,), (0,)), ((), ())), preferred_element_type=F32)
            return carry

        return lax.fori_loop(0, CHUNK // STEP, some, carry)

    lax.fori_loop(0, chunks, step, 0)
    for index, out in enumerate(outs):
        def put(at, carry, out=out, index=index):
            out[at] = total[8 * index + at].astype(BF16)
            return carry

        lax.fori_loop(0, 8, put, 0)


def backward(chunks, row_slot, col_slot, pieces, source, weights):
    slots = weights.shape[0]
    return pl.pallas_call(
        backward_kernel,
        out_shape=(shape((8, TS, H)), shape((8, TS, H)), shape(source.shape)),
        in_specs=[pl.BlockSpec(memory_space=pltpu.SMEM)] * 3 + vmem_specs(5) + [pl.BlockSpec(memory_space=pltpu.HBM)],
        out_specs=tuple(vmem_specs(3)),
        scratch_shapes=[
            VMEM(weights.shape, BF16),
            VMEM((17, TS, H), F32),
            pltpu.SemaphoreType.DMA((slots // CHUNK,)),
            pltpu.SemaphoreType.DMA((4,)),
        ],
        input_output_aliases={7: 2},
        compiler_params=params(20),
        cost_estimate=pl.CostEstimate(flops=slots * 2 * TS * TS * H, bytes_accessed=slots * TS * TS * 2, transcendentals=0),
        name="backward",
    )(chunks, row_slot, col_slot, *pieces, source, weights)[:2]


def fold_core_kernel(own_ref, got_ref, *outs):
    for index, out in enumerate(outs):
        at = index % 4 * 2 + index // 4
        out[...] = (own_ref[at].astype(F32) + got_ref[at].astype(F32)).astype(BF16)


def fold_core(own, got):
    return pl.pallas_call(
        fold_core_kernel,
        out_shape=tuple([shape((TS, H))] * 8),
        in_specs=vmem_specs(2),
        out_specs=tuple(vmem_specs(8)),
        compiler_params=params(8),
        name="fold_core",
    )(own, got)


def fold_y_kernel(p0, p1, p2, p3, out_ref):
    out_ref[...] = sum_refs((p0, p1, p2, p3), slice(None)).astype(BF16)


def fold_y(parts):
    return pl.pallas_call(
        fold_y_kernel,
        out_shape=shape((TS, H)),
        in_specs=vmem_specs(4),
        out_specs=pl.BlockSpec(memory_space=VMEM),
        compiler_params=params(8),
        name="fold_y",
    )(*parts)


def final_kernel(p0, p1, p2, p3, got_ref, scaled_ref, grad_ref, features_ref, cotangent_ref, out_ref):
    def body(rows):
        as_float = features_ref[rows, :].astype(F32)
        messages = softplus(as_float)
        powered = jnp.exp(EXPONENT * jnp.log(messages))
        back_sums = sum_refs((p0, p1, p2, p3, got_ref), (rows, slice(None)))
        grad_message = (scaled_ref[rows, :] + back_sums) * (EXPONENT * powered / messages) * sigmoid(as_float)
        out_ref[rows, :] = cotangent_ref[rows, :].astype(F32) + grad_ref[rows, :] + grad_message

    strips(body)


def final(parts, got, scaled, grad, features, cotangent):
    return pl.pallas_call(
        final_kernel,
        out_shape=shape((TS, H), F32),
        in_specs=vmem_specs(9),
        out_specs=pl.BlockSpec(memory_space=VMEM),
        compiler_params=params(8),
        name="final",
    )(*parts, got, scaled, grad, features, cotangent)


def direct(value, axis):
    return [value] + [shift(value, axis, step) for step in (1, 2, 3)]


def ring(value, axis):
    behind, ahead = shift(value, axis, 1), shift(value, axis, 3)
    return value, behind, shift(behind[:2], axis, 1), shift(ahead[2:], axis, 3), ahead


def ring_sums(slabs, axis, with_degree):
    own, behind, first, last, ahead = slabs
    got_first, got_last = shift(first, axis, 1), shift(last, axis, 3)
    behind, ahead = relay(behind, ahead, got_first, got_last, with_degree)
    return own, shift(behind, axis, 1), shift(ahead, axis, 3)


def spread(slabs, axis):
    return [slabs[0]] + [shift(slabs[step], axis, step) for step in (1, 2, 3)]


def local(features, cotangent, w_first, w_second, weights, tile_rows, tile_cols, tile_counts):
    slots = weights.shape[0]
    zh, core, zl, x, y = (lax.axis_index(axis) for axis in AXES)
    live = jnp.arange(slots, dtype=jnp.int32) < tile_counts[0]
    chunks = (tile_counts + CHUNK - 1) // CHUNK
    row_z, row_x, row_y = tile_rows // 16, tile_rows // 4 % 4, tile_rows % 4
    row_ahead = ((row_y - y) & 3) * 16 + ((row_x - x) & 3) * 4 + ((row_z - zl) & 3)
    row_behind = ((y - row_y) & 3) * 16 + ((x - row_x) & 3) * 4 + ((zl - row_z) & 3)
    col_h, col_core, col_y = tile_cols // 8, tile_cols // 4 % 2, tile_cols % 4
    col_base = (col_core ^ core) * 8 + (col_h ^ zh)
    row_total = jnp.where(live, row_ahead, 64)
    col_panel = col_base + ((y - col_y) & 3) * 2
    col_total = jnp.where(live, (col_core ^ core) * 8 + ((col_y - y) & 3) * 2 + (col_h ^ zh), 16)
    weights = pltpu.with_memory_space_constraint(weights, pltpu.HBM)

    far = swap(features, "zh")
    degree = degrees(chunks, row_total, weights)
    far, degree, col_panel = lax.optimization_barrier((far, degree, col_panel))
    panels = stack(direct(power(features, far), "y"))
    slabs = forward(chunks, row_total, col_panel, (panels, swap(panels, "core")), degree, weights)
    odd = (y & 1).astype(jnp.int32).reshape(1)
    slabs_a = fold(ring_sums(slabs[:5], "y", True), True)
    sums_b = add(pairwise(*pair(odd, ring_sums(slabs[5:], "x", False)), "y"))
    slabs = join(spread(slabs_a, "x"), sums_b)
    scaled, grad_mixed, scaled_half = terms(spread(slabs, "zl"), features, cotangent, w_first, w_second)

    rows_a, rows_b = halves(direct(scaled_half, "zl"))
    rows_a = stack(direct(rows_a, "x"))
    rows_b = stack(direct(rows_b, "y"))
    pieces = (*ring(rows_a, "y"), *ring(rows_b, "x"))
    source = place([pieces[at] for at in (0, 1, 4, 5, 6, 9)])
    pieces = [pieces[at] for at in (2, 3, 7, 8)]
    own, other = backward(chunks, row_behind, col_total, pieces, source, weights)
    slabs = fold_core(own, swap(other, "core"))
    far = fold_y(spread(slabs[4:], "y"))
    return final(spread(slabs[:4], "y"), swap(far, "zh"), scaled, grad_mixed, features, cotangent)


def solution(mesh):
    split = Mesh(mesh.devices.reshape(2, 2, 4, 4, 4), AXES)
    placed = (P(AXES, None), P(AXES, None), P(), P(), P(AXES, None, None), P(AXES), P(AXES), P(AXES))
    return jax.shard_map(local, mesh=split, in_specs=placed, out_specs=P(AXES, None), check_vma=False)
```
